32 devices in a mesh: seq: 8 (over z, y), head: 4 (over x, core).
Axes of the slice: x: 2, y: 2, z: 4, core: 2. Of those that a mesh axis runs over, the one named last changes fastest.
Arguments:
- q_in: bfloat16 [1024, 2048], P(('seq', 'head')), may hold values from -52 to 52
- k_in: bfloat16 [1024, 2048], P(('seq', 'head')), may hold values from -6 to 6
- v_in: bfloat16 [1024, 2048], P(('seq', 'head')), may hold values from -6 to 6
- grad_out: bfloat16 [1024, 2048], P(('seq', 'head')), may hold values from -6 to 6
- positions: int32 [3, 1024], P(None, 'seq'), may hold values from 0 to 79, as said below
- views: int32 [1024], replicated, may hold values from 0 to 5, as said below
- adjacency: int32 [6, 2], replicated, may hold values from 0 to 5, as said below
Outputs:
- attended: bfloat16 [1024, 2048], P('seq', 'head')
- grad_q: bfloat16 [1024, 2048], P('seq', 'head')
- grad_k: bfloat16 [1024, 2048], P('seq', 'head')
- grad_v: bfloat16 [1024, 2048], P('seq', 'head')
The draws below stay inside these ranges and needn't reach their ends.
Inputs may be any that keep to these rules, and one draw needn't show every extreme that they name: `positions`: time ids lie below 16, height ids below 44, width ids below 80. `views`: never decreasing, starting at 0; a view changes only at a multiple of 128 rows; each view holds the rows of 1 device or of one device more, and which views hold one more is drawn. `adjacency`: the two entries of a view are distinct other views; the relation is symmetric and joins all views in one closed cycle.
All inputs are finite; a program needn't handle non-finite values.
Results may differ from the reference program's by a relative error of at most 0.025.
Values may be sent and summed in bfloat16 or wider, within the bound.
No kernel may reach another device: no remote copies, remote signals or barrier semaphores. Data moves between devices by JAX's collectives and lax.ppermute only.
A program may use at most 64 MiB of HBM per device.

```python
import jax
import jax.numpy as jnp
from jax import lax

HD = 128
HEADS = 16
VIEWS = 6
TOK_DEV = 128
TOKENS = 1024


def query_key_pair(key):
    shape = (TOKENS, HEADS * HD)
    keys = jnp.clip(jax.random.normal(jax.random.fold_in(key, 11), shape, jnp.float32), -6.0, 6.0)
    queries = jnp.clip(jax.random.normal(jax.random.fold_in(key, 12), shape, jnp.float32), -6.0, 6.0)
    return (queries, keys)


def draw_q_in(key, part):
    return query_key_pair(key)[0].astype(jnp.bfloat16)


def draw_k_in(key, part):
    return query_key_pair(key)[1].astype(jnp.bfloat16)


def draw_positions(key, part):
    frames = jax.random.randint(jax.random.fold_in(key, 31), (TOKENS,), 0, 16, jnp.int32)
    height = jax.random.randint(jax.random.fold_in(key, 32), (TOKENS,), 0, 44, jnp.int32)
    width = jax.random.randint(jax.random.fold_in(key, 33), (TOKENS,), 0, 80, jnp.int32)
    stacked = jnp.stack([frames, height, width], axis=0)
    stacked = stacked.at[:, TOKENS // 2].set(jnp.array([15, 43, 79], jnp.int32))
    stacked = stacked.at[:, 0].set(jnp.zeros((3,), jnp.int32))
    return stacked


def draw_views(key, part):
    devices = TOKENS // TOK_DEV
    order = jax.random.permutation(jax.random.fold_in(key, 41), VIEWS).astype(jnp.int32)
    extra = (order < devices % VIEWS).astype(jnp.int32)
    counts = devices // VIEWS + extra
    ends = jnp.cumsum(counts).astype(jnp.int32)
    device_of = (jnp.arange(TOKENS, dtype=jnp.int32) // TOK_DEV).astype(jnp.int32)
    return jnp.sum((device_of[:, None] >= ends[None, :]).astype(jnp.int32), axis=1).astype(jnp.int32)


def draw_adjacency(key, part):
    order = jax.random.permutation(jax.random.fold_in(key, 21), VIEWS).astype(jnp.int32)
    before = jnp.roll(order, 1)
    after = jnp.roll(order, -1)
    table = jnp.zeros((VIEWS, 2), jnp.int32)
    return table.at[order].set(jnp.stack([before, after], axis=1))


def steps_of(stream_key, extent, shards, smallest, high):
    loudness = 1.0
    for axis_at, blocks in shards:
        steps = jax.random.uniform(jax.random.fold_in(jax.random.fold_in(stream_key, 6), axis_at), (blocks,), jnp.float32, smallest / len(shards), high / len(shards))
        loudness = loudness * jnp.repeat(jnp.exp(steps), extent[axis_at] // blocks).reshape((-1,) + (1,) * (len(extent) - 1 - axis_at))
    return loudness


def noise(own_key, shape, scale, bound, shards=(), kind=jnp.bfloat16):
    result = scale * jax.random.normal(own_key, shape, jnp.float32)
    if shards:
        result = result * steps_of(own_key, shape, shards, -0.22, 0.18)
    return jnp.clip(result, -bound, bound).astype(kind)


def setup_inputs(seed: int = 0) -> dict:
    splits = jax.random.split(jax.random.key(seed), 8)
    q_in = draw_q_in(jax.random.fold_in(splits[7], 71), 0)
    k_in = draw_k_in(jax.random.fold_in(splits[7], 71), 0)
    v_in = noise(splits[2], (TOKENS, HEADS * HD), 1.0, 6.0, ((0, 32),))
    grad_out = noise(splits[3], (TOKENS, HEADS * HD), 1.0, 6.0, ((0, 32),))
    positions = draw_positions(jax.random.fold_in(splits[7], 71), 0)
    views = draw_views(jax.random.fold_in(splits[7], 71), 0)
    adjacency = draw_adjacency(jax.random.fold_in(splits[7], 71), 0)
    return dict(q_in=q_in, k_in=k_in, v_in=v_in, grad_out=grad_out, positions=positions, views=views, adjacency=adjacency)


NEG = -1e30
THETA = 10000.0


def rope_tables(positions, width):
    side = width // 6 * 2
    first = width - 2 * side
    parts = []
    for row, group in ((0, first), (1, side), (2, side)):
        steps = jnp.arange(group // 2, dtype=jnp.float32)
        inverse = THETA ** (-2.0 * steps / group)
        parts.append(positions[row].astype(jnp.float32)[:, None] * inverse[None, :])
    angles = jnp.concatenate(parts, axis=1)
    return jnp.cos(angles), jnp.sin(angles)


def rotate(values, cosine, sine, sign):
    half = values.shape[-1] // 2
    first = values[..., :half]
    second = values[..., half:]
    return jnp.concatenate([first * cosine - sign * second * sine, sign * first * sine + second * cosine], axis=-1)


def neighbours(view_ids, adjacency):
    count = adjacency.shape[0]
    match = view_ids[:, None] == jnp.arange(count, dtype=jnp.int32)[None, :]
    near_one = jnp.sum(jnp.where(match, adjacency[None, :, 0], 0), axis=1).astype(jnp.int32)
    near_two = jnp.sum(jnp.where(match, adjacency[None, :, 1], 0), axis=1).astype(jnp.int32)
    return near_one, near_two


def reference(q_in, k_in, v_in, grad_out, positions, views, adjacency):
    scale = HD ** -0.5
    cosine, sine = rope_tables(positions, HD)
    near_one, near_two = neighbours(views, adjacency)
    other = views[None, :]
    allowed = (other == views[:, None]) | (other == near_one[:, None]) | (other == near_two[:, None])

    def one_head(head):
        start = head * HD

        def take(array):
            return lax.dynamic_slice_in_dim(array, start, HD, 1)

        query = rotate(take(q_in).astype(jnp.float32), cosine, sine, 1.0).astype(jnp.bfloat16)
        keyrot = rotate(take(k_in).astype(jnp.float32), cosine, sine, 1.0).astype(jnp.bfloat16)
        values = take(v_in)
        grads = take(grad_out)
        scores = jnp.dot(query, keyrot.T, preferred_element_type=jnp.float32) * scale
        scores = jnp.where(allowed, scores, NEG)
        top = jnp.max(scores, axis=1)
        weights = jnp.where(allowed, jnp.exp(scores - top[:, None]), 0.0)
        total = jnp.sum(weights, axis=1)
        output = jnp.dot(weights.astype(jnp.bfloat16), values, preferred_element_type=jnp.float32) / total[:, None]
        level = top + jnp.log(total)
        delta = jnp.sum(grads.astype(jnp.float32) * output, axis=1)
        probs = jnp.where(allowed, jnp.exp(scores - level[:, None]), 0.0)
        dprobs = jnp.dot(grads, values.T, preferred_element_type=jnp.float32)
        dscores = (probs * (dprobs - delta[:, None])).astype(jnp.bfloat16)
        grad_query = jnp.dot(dscores, keyrot, preferred_element_type=jnp.float32) * scale
        grad_key = jnp.dot(dscores.T, query, preferred_element_type=jnp.float32) * scale
        grad_value = jnp.dot(probs.astype(jnp.bfloat16).T, grads, preferred_element_type=jnp.float32)
        return (output.astype(jnp.bfloat16),
                rotate(grad_query, cosine, sine, -1.0).astype(jnp.bfloat16),
                rotate(grad_key, cosine, sine, -1.0).astype(jnp.bfloat16),
                grad_value.astype(jnp.bfloat16))

    results = lax.map(one_head, jnp.arange(HEADS, dtype=jnp.int32))

    def merge_heads(stack):
        return jnp.transpose(stack, (1, 0, 2)).reshape(TOKENS, HEADS * HD)

    return (merge_heads(results[0]), merge_heads(results[1]), merge_heads(results[2]), merge_heads(results[3]))
```

```python
import functools
import math

import jax
import jax.numpy as jnp
import numpy as np
from jax import lax
from jax.experimental import pallas as pl
from jax.experimental.pallas import tpu as pltpu
from jax.sharding import PartitionSpec as P

HD = 128


NEG = -1e30
THETA = 10000.0


def rope_tables(positions, width):
    side = width // 6 * 2
    first = width - 2 * side
    parts = []
    for row, group in ((0, first), (1, side), (2, side)):
        steps = jnp.arange(group // 2, dtype=jnp.float32)
        inverse = THETA ** (-2.0 * steps / group)
        parts.append(positions[row].astype(jnp.float32)[:, None] * inverse[None, :])
    angles = jnp.concatenate(parts, axis=1)
    return (jnp.cos(angles), jnp.sin(angles))


def rotate(values, cosine, sine, sign):
    half = values.shape[-1] // 2
    first = values[..., :half]
    second = values[..., half:]
    return jnp.concatenate(
        [first * cosine - sign * second * sine, sign * first * sine + second * cosine], axis=-1
    )


def neighbours(view_ids, adjacency):
    count = adjacency.shape[0]
    match = view_ids[:, None] == jnp.arange(count, dtype=jnp.int32)[None, :]
    near_one = jnp.sum(jnp.where(match, adjacency[None, :, 0], 0), axis=1)
    near_two = jnp.sum(jnp.where(match, adjacency[None, :, 1], 0), axis=1)
    return (near_one, near_two)


def in_blocks(pieces, carry, step):
    count = pieces[0].shape[0]
    size = count
    while size > 1024 and size % 2 == 0:
        size = size // 2
    number = count // size
    shaped = tuple((piece.reshape((number, size) + piece.shape[1:]) for piece in pieces))
    firsts = size * jnp.arange(number, dtype=jnp.int32)

    def advance(state, item):
        return (step(state, item[0], item[1]), None)

    final, _ = lax.scan(advance, carry, (shaped, firsts))
    return final


def on_device(q_in, k_in, v_in, grad_out, positions, views, adjacency):
    query, keys, values, grads = (
        lax.all_to_all(q_in, "head", split_axis=1, concat_axis=0, tiled=True),
        lax.all_to_all(k_in, "head", split_axis=1, concat_axis=0, tiled=True),
        lax.all_to_all(v_in, "head", split_axis=1, concat_axis=0, tiled=True),
        lax.all_to_all(grad_out, "head", split_axis=1, concat_axis=0, tiled=True),
    )
    rows, width = query.shape
    heads = width // HD
    scale = HD ** (-0.5)
    cosine, sine = rope_tables(positions, HD)
    cosine = cosine[:, None, :]
    sine = sine[:, None, :]
    query_rot = rotate(
        query.reshape(rows, heads, HD).astype(jnp.float32), cosine, sine, 1.0
    ).astype(jnp.bfloat16)
    key_rot = rotate(keys.reshape(rows, heads, HD).astype(jnp.float32), cosine, sine, 1.0).astype(
        jnp.bfloat16
    )
    value_split = values.reshape(rows, heads, HD)
    grad_split = grads.reshape(rows, heads, HD)
    first_row = lax.axis_index("seq") * rows
    own_views = lax.dynamic_slice_in_dim(views, first_row, rows)
    near_one, near_two = neighbours(own_views, adjacency)
    every_one, every_two = neighbours(views, adjacency)

    def allowed_keys(start, count):
        other = lax.dynamic_slice_in_dim(views, start, count)[None, :]
        return (
            (other == own_views[:, None])
            | (other == near_one[:, None])
            | (other == near_two[:, None])
        )

    def scores_for(key_block, allow):
        scores = (
            jnp.einsum("qhd,khd->hqk", query_rot, key_block, preferred_element_type=jnp.float32)
            * scale
        )
        return jnp.where(allow[None], scores, NEG)

    def soft_update(top, total, accum, block, start):
        key_block, value_block = block
        allow = allowed_keys(start, key_block.shape[0])
        scores = scores_for(key_block, allow)
        new_top = jnp.maximum(top, jnp.max(scores, axis=2))
        shrink = jnp.exp(top - new_top)
        weights = jnp.where(allow[None], jnp.exp(scores - new_top[..., None]), 0.0)
        total = total * shrink + jnp.sum(weights, axis=2)
        accum = accum * shrink[..., None] + jnp.einsum(
            "hqk,khd->hqd",
            weights.astype(jnp.bfloat16),
            value_block,
            preferred_element_type=jnp.float32,
        )
        return (new_top, total, accum, weights, shrink)

    top_init = jnp.full((heads, rows), NEG, jnp.float32)
    total_init = jnp.zeros((heads, rows), jnp.float32)
    accum_init = jnp.zeros((heads, rows, HD), jnp.float32)

    def step(inner, block, bstart):
        top, total, accum, weights, shrink = soft_update(
            inner[0], inner[1], inner[2], block, bstart
        )
        return (top, total, accum)

    top, total, accum = in_blocks(
        (
            lax.all_gather(key_rot, "seq", axis=0, tiled=True),
            lax.all_gather(value_split, "seq", axis=0, tiled=True),
        ),
        (top_init, total_init, accum_init),
        step,
    )
    output = accum / total[..., None]
    finish_level = top + jnp.log(total)
    finish_delta = jnp.sum(
        grad_split.astype(jnp.float32) * jnp.transpose(output, (1, 0, 2)), axis=2
    ).T
    output, level, delta = (output, finish_level, finish_delta)

    def step(inner, block, bstart):
        key_block, value_block = block
        allow = allowed_keys(bstart, key_block.shape[0])
        scores = scores_for(key_block, allow)
        probs = jnp.where(allow[None], jnp.exp(scores - level[..., None]), 0.0)
        dprobs = jnp.einsum(
            "qhd,khd->hqk", grad_split, value_block, preferred_element_type=jnp.float32
        )
        dscores = (probs * (dprobs - delta[..., None])).astype(jnp.bfloat16)
        return inner + jnp.einsum(
            "hqk,khd->hqd", dscores, key_block, preferred_element_type=jnp.float32
        )

    grad_query = (
        in_blocks(
            (
                lax.all_gather(key_rot, "seq", axis=0, tiled=True),
                lax.all_gather(value_split, "seq", axis=0, tiled=True),
            ),
            accum_init,
            step,
        )
        * scale
    )
    level_all, delta_all = (
        lax.all_gather(level.T, "seq", axis=0, tiled=True),
        lax.all_gather(delta.T, "seq", axis=0, tiled=True),
    )

    def step(inner, block, bstart):
        grad_key, grad_value = inner
        query_block, grad_block = block
        count = query_block.shape[0]
        query_views = lax.dynamic_slice_in_dim(views, bstart, count)[None, :]
        query_one = lax.dynamic_slice_in_dim(every_one, bstart, count)[None, :]
        query_two = lax.dynamic_slice_in_dim(every_two, bstart, count)[None, :]
        mine = own_views[:, None]
        allow = (mine == query_views) | (mine == query_one) | (mine == query_two)
        level_block = lax.dynamic_slice_in_dim(level_all, bstart, count).T
        delta_block = lax.dynamic_slice_in_dim(delta_all, bstart, count).T
        scores = (
            jnp.einsum("khd,qhd->hkq", key_rot, query_block, preferred_element_type=jnp.float32)
            * scale
        )
        probs = jnp.where(allow[None], jnp.exp(scores - level_block[:, None, :]), 0.0)
        grad_value = grad_value + jnp.einsum(
            "hkq,qhd->hkd",
            probs.astype(jnp.bfloat16),
            grad_block,
            preferred_element_type=jnp.float32,
        )
        dprobs = jnp.einsum(
            "khd,qhd->hkq", value_split, grad_block, preferred_element_type=jnp.float32
        )
        dscores = (probs * (dprobs - delta_block[:, None, :])).astype(jnp.bfloat16)
        grad_key = grad_key + jnp.einsum(
            "hkq,qhd->hkd", dscores, query_block, preferred_element_type=jnp.float32
        )
        return (grad_key, grad_value)

    grad_key, grad_value = in_blocks(
        (
            lax.all_gather(query_rot, "seq", axis=0, tiled=True),
            lax.all_gather(grad_split, "seq", axis=0, tiled=True),
        ),
        (accum_init, accum_init),
        step,
    )

    def token_major(stack):
        return jnp.transpose(stack, (1, 0, 2))

    attended = token_major(output).reshape(rows, width).astype(jnp.bfloat16)
    grad_q = (
        rotate(token_major(grad_query), cosine, sine, -1.0)
        .reshape(rows, width)
        .astype(jnp.bfloat16)
    )
    grad_k = (
        rotate(token_major(grad_key) * scale, cosine, sine, -1.0)
        .reshape(rows, width)
        .astype(jnp.bfloat16)
    )
    grad_v = token_major(grad_value).reshape(rows, width).astype(jnp.bfloat16)
    return (attended, grad_q, grad_k, grad_v)


LOG2E = math.log2(math.e)
VMEM_LIMIT = 48 * 1024 * 1024
PAD = 3


def whole(space=pltpu.VMEM):
    return pl.BlockSpec(memory_space=space)


def inverse_steps():
    side = HD // 6 * 2
    first = HD - 2 * side
    parts, rows = [], []
    for row, group in ((0, first), (1, side), (2, side)):
        steps = np.arange(group // 2, dtype=np.float64)
        parts.append(THETA ** (-2.0 * steps / group))
        rows.append(np.full(group // 2, row))
    table = np.zeros((HD // 2, 8), np.float32)
    table[np.arange(HD // 2), np.concatenate(rows)] = np.concatenate(parts)
    return table


def prepare_kernel(row_first, head_of, pos_ref, step_ref, q_ref, k_ref, v_ref, g_ref, out_ref, table_ref):
    rows = q_ref.shape[0]
    angle = (
        step_ref[:, 0:1] * pos_ref[0:1, :].astype(jnp.float32)
        + step_ref[:, 1:2] * pos_ref[1:2, :].astype(jnp.float32)
        + step_ref[:, 2:3] * pos_ref[2:3, :].astype(jnp.float32)
    )
    cosine, sine = jnp.cos(angle), jnp.sin(angle)
    table_ref[0] = jnp.concatenate([cosine, cosine], axis=0).T
    table_ref[1] = jnp.concatenate([-sine, sine], axis=0).T
    own = pl.ds(pl.multiple_of(row_first() * rows, rows), rows)
    cosine, sine = table_ref[0, own, :], table_ref[1, own, :]
    for chip, head in enumerate(head_of):
        lanes = slice(head * HD, (head + 1) * HD)
        for at, ref in ((0, q_ref), (1, k_ref)):
            x = ref[:, lanes].astype(jnp.float32)
            out_ref[chip, at * rows : (at + 1) * rows, :] = (
                x * cosine + pltpu.roll(x, HD // 2, 1) * sine
            ).astype(jnp.bfloat16)
        out_ref[chip, 2 * rows : 3 * rows, :] = v_ref[:, lanes]
        out_ref[chip, 3 * rows : 4 * rows, :] = g_ref[:, lanes]


def attend_kernel(
    core_of, views_ref, near_ref, mine_ref, other_ref, out_ref,
    q_all, g_all, k_all, v_all, kt_all, vt_all, s_all, d_all, p_all, ds_all, dk_all, dv_all, order, rank,
):
    blocks = out_ref.shape[0]
    half = out_ref.shape[1] // 4
    rows = half // 2
    block = 2 * half
    count = near_ref.shape[0]
    span = count_span(count, blocks)
    wide = 2 * block
    core = core_of()
    scale = HD**-0.5
    first, held = [], []
    for view in range(count):
        below, equal = 0, 0
        for b in range(blocks):
            below = below + (views_ref[b * block] < view).astype(jnp.int32)
            equal = equal + (views_ref[b * block] == view).astype(jnp.int32)
        first.append(below)
        held.append(equal)

    def pick(table, at):
        value = table[0]
        for view in range(1, count):
            value = jnp.where(at == view, table[view], value)
        return value

    last, now, place = jnp.int32(0), near_ref[0, 0], jnp.int32(0)
    start, size = [], []
    cycle = [last, now]
    for _ in range(count - 2):
        one, two = near_ref[now, 0], near_ref[now, 1]
        last, now = now, jnp.where(one == last, two, one)
        cycle.append(now)
    for i, view in enumerate(cycle):
        f, n = pick(first, view), pick(held, view)
        start.append(place)
        size.append(n)
        for extra in range(2):
            order[place + extra] = f + extra
            rank[place + extra] = jnp.int32(i)
        place = place + n
    for pos in range(blocks):
        src = order[pos]
        spots = [pos + PAD]
        if pos - blocks + PAD >= 0:
            spots.append(pos - blocks + PAD)
        if pos + blocks + PAD < blocks + 2 * PAD:
            spots.append(pos + blocks + PAD)

        def take(at):
            part = slice(at * rows, (at + 1) * rows)
            return jnp.concatenate(
                [mine_ref[2 * src, part, :], mine_ref[2 * src + 1, part, :],
                 other_ref[2 * src, part, :], other_ref[2 * src + 1, part, :]], axis=0)

        tile, at = pos // 2, pos % 2
        for ref, source in ((q_all, take(0)), (g_all, take(3))):
            base = tile * wide + at * half
            ref[base : base + half, :] = source[:half]
            ref[base + block : base + block + half, :] = source[half:]
        for ref, turned, source in ((k_all, kt_all, take(1)), (v_all, vt_all, take(2))):
            across = source.astype(jnp.float32).T.astype(jnp.bfloat16)
            for spot in spots:
                ref[spot * block : (spot + 1) * block, :] = source
                if turned is kt_all:
                    turned[:, spot * block : (spot + 1) * block] = across
                else:
                    turned[:, spot * block : (spot + 1) * block] = across
    dk_all[...] = jnp.zeros_like(dk_all)
    dv_all[...] = jnp.zeros_like(dv_all)

    nt = (((1,), (1,)), ((), ()))
    lane = lax.broadcasted_iota(jnp.int32, (1, wide), 1)
    second = (lane // half) % 2 == 1

    for tile in range(blocks // 2):
        rank_a, rank_b = rank[2 * tile], rank[2 * tile + 1]
        before = lax.rem(rank_a + count - 1, count)
        begin = pick(start, rank_a) - pick(size, before) + PAD
        window = pl.ds(pl.multiple_of(begin * block, block), span * block)
        q_tile = q_all[tile * wide : (tile + 1) * wide, :]
        g_tile = g_all[tile * wide : (tile + 1) * wide, :]
        s_all[...] = lax.dot_general(k_all[window, :], q_tile, nt, preferred_element_type=jnp.float32)
        d_all[...] = lax.dot_general(v_all[window, :], g_tile, nt, preferred_element_type=jnp.float32)
        top = jnp.full((1, wide), NEG, jnp.float32)
        oks = []
        for i in range(span):
            at = lax.rem(begin - PAD + i + blocks, blocks)
            key_rank = rank[at]
            far_a = lax.rem(key_rank - rank_a + count, count)
            far_b = lax.rem(key_rank - rank_b + count, count)
            ok_a = ((far_a <= 1) | (far_a == count - 1)).astype(jnp.int32)
            ok_b = ((far_b <= 1) | (far_b == count - 1)).astype(jnp.int32)
            ok = jnp.where(second, ok_b, ok_a) > 0
            oks.append(ok)
            part = jnp.where(ok, s_all[i * block : (i + 1) * block, :], NEG)
            top = jnp.maximum(top, jnp.max(part, axis=0, keepdims=True))
        factor = scale * LOG2E
        level = top * factor
        total = jnp.zeros((1, wide), jnp.float32)
        delta = jnp.zeros((1, wide), jnp.float32)
        for i in range(span):
            here = slice(i * block, (i + 1) * block)
            e = jnp.where(oks[i], jnp.exp2(s_all[here, :] * factor - level), 0.0)
            s_all[here, :] = e
            total = total + jnp.sum(e, axis=0, keepdims=True)
            delta = delta + jnp.sum(e * d_all[here, :], axis=0, keepdims=True)
            ds_all[here, :] = e.astype(jnp.bfloat16)
        share = 1.0 / total
        delta = delta * share
        out_t = jnp.dot(vt_all[:, window], ds_all[:, :block], preferred_element_type=jnp.float32)
        out = (out_t * share[:, :block]).T.astype(jnp.bfloat16)
        for i in range(span):
            here = slice(i * block, (i + 1) * block)
            p = s_all[here, :] * share
            p_all[i, :, :] = p[:half].astype(jnp.bfloat16)
            ds_all[here, :] = (p * (d_all[here, :] - delta)).astype(jnp.bfloat16)
        dq_t = jnp.dot(kt_all[:, window], ds_all[:, :block], preferred_element_type=jnp.float32)
        dq = (dq_t * scale).T.astype(jnp.bfloat16)
        own = pl.ds(pl.multiple_of(begin * half, half), span * half)
        dv_all[own, :] += jnp.dot(p_all[...].reshape(span * half, wide), g_tile, preferred_element_type=jnp.float32)
        mine_ds = ds_all[...].reshape(span, block, wide)[:, :half].reshape(span * half, wide)
        dk_all[own, :] += jnp.dot(mine_ds, q_tile, preferred_element_type=jnp.float32)
        for at in range(2):
            src = order[2 * tile + at]
            to = src // 2 + (blocks // 2) * (lax.rem(src, 2) != core).astype(jnp.int32)
            out_ref[to, 0:half, :] = out[at * half : (at + 1) * half]
            out_ref[to, half : 2 * half, :] = dq[at * half : (at + 1) * half]
    for pos in range(blocks):
        src = order[pos]
        to = src // 2 + (blocks // 2) * (lax.rem(src, 2) != core).astype(jnp.int32)
        spots = [pos + PAD]
        if pos - blocks + PAD >= 0:
            spots.append(pos - blocks + PAD)
        if pos + blocks + PAD < blocks + 2 * PAD:
            spots.append(pos + blocks + PAD)
        dk = sum(dk_all[spot * half : (spot + 1) * half, :] for spot in spots)
        dv = sum(dv_all[spot * half : (spot + 1) * half, :] for spot in spots)
        out_ref[to, 2 * half : 3 * half, :] = (dk * scale).astype(jnp.bfloat16)
        out_ref[to, 3 * half : 4 * half, :] = dv.astype(jnp.bfloat16)


def finish_kernel(core_of, table_ref, keep_ref, swap_ref, att_ref, dq_ref, dk_ref, dv_ref):
    heads = swap_ref.shape[0]
    half = keep_ref.shape[1] // 4
    rows = half // 2
    core = core_of()
    for ref, which in ((keep_ref, core), (swap_ref, 1 - core)):
        for pair in range(2):
            there = pl.ds(pl.multiple_of(pair * half + which * rows, rows), rows)
            cosine, sine = table_ref[0, there, :], table_ref[1, there, :]
            for head in range(heads):
                lanes = slice(head * HD, (head + 1) * HD)
                for at, out in ((0, att_ref), (1, dq_ref), (2, dk_ref), (3, dv_ref)):
                    x = ref[head, at * half + pair * rows : at * half + (pair + 1) * rows, :]
                    if at in (1, 2):
                        x = x.astype(jnp.float32)
                        x = x * cosine - pltpu.roll(x, HD // 2, 1) * sine
                        x = x.astype(jnp.bfloat16)
                    out[there, lanes] = x


def count_span(count, blocks):
    return 4 + blocks - count


def by_chip(seqs, parts, q_in, k_in, v_in, grad_out, positions, views, adjacency):
    rows, width = q_in.shape
    heads = width // HD
    xs = parts // 2
    group = heads // parts
    chips = seqs * xs
    block = rows * parts
    half = block // 2
    count = adjacency.shape[0]
    span = count_span(count, seqs)
    long = seqs + 2 * PAD
    wide = 2 * block
    head_of = [((c % xs) * 2 + (c // xs) % 2) * group + c // xs // 2 for c in range(chips)]
    limits = pltpu.CompilerParams(vmem_limit_bytes=VMEM_LIMIT)

    def row_first():
        return lax.axis_index("head")

    def core_of():
        return lax.rem(lax.axis_index("head"), 2)

    sent, table = pl.pallas_call(
        functools.partial(prepare_kernel, row_first, head_of),
        out_shape=(
            jax.ShapeDtypeStruct((chips, 4 * rows, HD), jnp.bfloat16),
            jax.ShapeDtypeStruct((2, block, HD), jnp.float32),
        ),
        in_specs=[whole()] * 6,
        out_specs=(whole(), whole()),
        compiler_params=limits,
        name="prepare",
    )(positions, jnp.asarray(inverse_steps()), q_in, k_in, v_in, grad_out)
    axes = ("seq", "head")
    same_core = [[(c // xs) * parts + (c % xs) * 2 + core for c in range(chips)] for core in range(2)]
    mine = lax.all_to_all(sent, axes, 0, 0, axis_index_groups=same_core, tiled=True)
    partner = [(d, d ^ 1) for d in range(seqs * parts)]
    other = lax.ppermute(mine, axes, partner)
    back = pl.pallas_call(
        functools.partial(attend_kernel, core_of),
        out_shape=jax.ShapeDtypeStruct((seqs, 4 * half, HD), jnp.bfloat16),
        in_specs=[whole(pltpu.SMEM), whole(pltpu.SMEM), whole(), whole()],
        out_specs=whole(),
        scratch_shapes=[
            pltpu.VMEM((seqs * block, HD), jnp.bfloat16),
            pltpu.VMEM((seqs * block, HD), jnp.bfloat16),
            pltpu.VMEM((long * block, HD), jnp.bfloat16),
            pltpu.VMEM((long * block, HD), jnp.bfloat16),
            pltpu.VMEM((HD, long * block), jnp.bfloat16),
            pltpu.VMEM((HD, long * block), jnp.bfloat16),
            pltpu.VMEM((span * block, wide), jnp.float32),
            pltpu.VMEM((span * block, wide), jnp.float32),
            pltpu.VMEM((span, half, wide), jnp.bfloat16),
            pltpu.VMEM((span * block, wide), jnp.bfloat16),
            pltpu.VMEM((long * half, HD), jnp.float32),
            pltpu.VMEM((long * half, HD), jnp.float32),
            pltpu.SMEM((seqs + 1,), jnp.int32),
            pltpu.SMEM((seqs + 1,), jnp.int32),
        ],
        compiler_params=limits,
        name="attend",
    )(views, adjacency, mine, other)
    ranked = [[s for s in range(seqs) if s % 2 == core] + [s for s in range(seqs) if s % 2 != core] for core in range(2)]
    along = [[s * parts + x * 2 + core for s in ranked[core]] for x in range(xs) for core in range(2)]
    keep = lax.all_to_all(back, axes, 0, 0, axis_index_groups=along, tiled=True)
    swap = lax.ppermute(keep[seqs // 2 :], axes, partner)
    return pl.pallas_call(
        functools.partial(finish_kernel, core_of),
        out_shape=(jax.ShapeDtypeStruct((block, group * HD), jnp.bfloat16),) * 4,
        in_specs=[whole()] * 3,
        out_specs=(whole(),) * 4,
        compiler_params=limits,
        name="finish",
    )(table, keep, swap)


def solution(mesh):
    seqs, parts = mesh.shape["seq"], mesh.shape["head"]
    in_specs = (
        P(("seq", "head"), None),
        P(("seq", "head"), None),
        P(("seq", "head"), None),
        P(("seq", "head"), None),
        P(None, "seq"),
        P(),
        P(),
    )
    out_specs = (P("seq", "head"), P("seq", "head"), P("seq", "head"), P("seq", "head"))

    def run(*args):
        heads = args[0].shape[1] // HD
        count = args[6].shape[0]
        fits = (
            seqs * parts == 2 * heads
            and seqs % 2 == 0
            and parts % 2 == 0
            and count <= seqs < 2 * count
            and count_span(count, seqs) <= seqs
        )
        step = functools.partial(by_chip, seqs, parts) if fits else on_device
        return jax.shard_map(
            step, mesh=mesh, in_specs=in_specs, out_specs=out_specs, check_vma=False
        )(*args)

    return run
```

```python
import functools
import math

import jax
import jax.numpy as jnp
import numpy as np
from jax import lax
from jax.experimental import pallas as pl
from jax.experimental.pallas import tpu as pltpu
from jax.sharding import PartitionSpec as P

HD = 128


NEG = -1e30
THETA = 10000.0


def rope_tables(positions, width):
    side = width // 6 * 2
    first = width - 2 * side
    parts = []
    for row, group in ((0, first), (1, side), (2, side)):
        steps = jnp.arange(group // 2, dtype=jnp.float32)
        inverse = THETA ** (-2.0 * steps / group)
        parts.append(positions[row].astype(jnp.float32)[:, None] * inverse[None, :])
    angles = jnp.concatenate(parts, axis=1)
    return (jnp.cos(angles), jnp.sin(angles))


def rotate(values, cosine, sine, sign):
    half = values.shape[-1] // 2
    first = values[..., :half]
    second = values[..., half:]
    return jnp.concatenate(
        [first * cosine - sign * second * sine, sign * first * sine + second * cosine], axis=-1
    )


def neighbours(view_ids, adjacency):
    count = adjacency.shape[0]
    match = view_ids[:, None] == jnp.arange(count, dtype=jnp.int32)[None, :]
    near_one = jnp.sum(jnp.where(match, adjacency[None, :, 0], 0), axis=1)
    near_two = jnp.sum(jnp.where(match, adjacency[None, :, 1], 0), axis=1)
    return (near_one, near_two)


def in_blocks(pieces, carry, step):
    count = pieces[0].shape[0]
    size = count
    while size > 1024 and size % 2 == 0:
        size = size // 2
    number = count // size
    shaped = tuple((piece.reshape((number, size) + piece.shape[1:]) for piece in pieces))
    firsts = size * jnp.arange(number, dtype=jnp.int32)

    def advance(state, item):
        return (step(state, item[0], item[1]), None)

    final, _ = lax.scan(advance, carry, (shaped, firsts))
    return final


def on_device(q_in, k_in, v_in, grad_out, positions, views, adjacency):
    query, keys, values, grads = (
        lax.all_to_all(q_in, "head", split_axis=1, concat_axis=0, tiled=True),
        lax.all_to_all(k_in, "head", split_axis=1, concat_axis=0, tiled=True),
        lax.all_to_all(v_in, "head", split_axis=1, concat_axis=0, tiled=True),
        lax.all_to_all(grad_out, "head", split_axis=1, concat_axis=0, tiled=True),
    )
    rows, width = query.shape
    heads = width // HD
    scale = HD ** (-0.5)
    cosine, sine = rope_tables(positions, HD)
    cosine = cosine[:, None, :]
    sine = sine[:, None, :]
    query_rot = rotate(
        query.reshape(rows, heads, HD).astype(jnp.float32), cosine, sine, 1.0
    ).astype(jnp.bfloat16)
    key_rot = rotate(keys.reshape(rows, heads, HD).astype(jnp.float32), cosine, sine, 1.0).astype(
        jnp.bfloat16
    )
    value_split = values.reshape(rows, heads, HD)
    grad_split = grads.reshape(rows, heads, HD)
    first_row = lax.axis_index("seq") * rows
    own_views = lax.dynamic_slice_in_dim(views, first_row, rows)
    near_one, near_two = neighbours(own_views, adjacency)
    every_one, every_two = neighbours(views, adjacency)

    def allowed_keys(start, count):
        other = lax.dynamic_slice_in_dim(views, start, count)[None, :]
        return (
            (other == own_views[:, None])
            | (other == near_one[:, None])
            | (other == near_two[:, None])
        )

    def scores_for(key_block, allow):
        scores = (
            jnp.einsum("qhd,khd->hqk", query_rot, key_block, preferred_element_type=jnp.float32)
            * scale
        )
        return jnp.where(allow[None], scores, NEG)

    def soft_update(top, total, accum, block, start):
        key_block, value_block = block
        allow = allowed_keys(start, key_block.shape[0])
        scores = scores_for(key_block, allow)
        new_top = jnp.maximum(top, jnp.max(scores, axis=2))
        shrink = jnp.exp(top - new_top)
        weights = jnp.where(allow[None], jnp.exp(scores - new_top[..., None]), 0.0)
        total = total * shrink + jnp.sum(weights, axis=2)
        accum = accum * shrink[..., None] + jnp.einsum(
            "hqk,khd->hqd",
            weights.astype(jnp.bfloat16),
            value_block,
            preferred_element_type=jnp.float32,
        )
        return (new_top, total, accum, weights, shrink)

    top_init = jnp.full((heads, rows), NEG, jnp.float32)
    total_init = jnp.zeros((heads, rows), jnp.float32)
    accum_init = jnp.zeros((heads, rows, HD), jnp.float32)

    def step(inner, block, bstart):
        top, total, accum, weights, shrink = soft_update(
            inner[0], inner[1], inner[2], block, bstart
        )
        return (top, total, accum)

    top, total, accum = in_blocks(
        (
            lax.all_gather(key_rot, "seq", axis=0, tiled=True),
            lax.all_gather(value_split, "seq", axis=0, tiled=True),
        ),
        (top_init, total_init, accum_init),
        step,
    )
    output = accum / total[..., None]
    finish_level = top + jnp.log(total)
    finish_delta = jnp.sum(
        grad_split.astype(jnp.float32) * jnp.transpose(output, (1, 0, 2)), axis=2
    ).T
    output, level, delta = (output, finish_level, finish_delta)

    def step(inner, block, bstart):
        key_block, value_block = block
        allow = allowed_keys(bstart, key_block.shape[0])
        scores = scores_for(key_block, allow)
        probs = jnp.where(allow[None], jnp.exp(scores - level[..., None]), 0.0)
        dprobs = jnp.einsum(
            "qhd,khd->hqk", grad_split, value_block, preferred_element_type=jnp.float32
        )
        dscores = (probs * (dprobs - delta[..., None])).astype(jnp.bfloat16)
        return inner + jnp.einsum(
            "hqk,khd->hqd", dscores, key_block, preferred_element_type=jnp.float32
        )

    grad_query = (
        in_blocks(
            (
                lax.all_gather(key_rot, "seq", axis=0, tiled=True),
                lax.all_gather(value_split, "seq", axis=0, tiled=True),
            ),
            accum_init,
            step,
        )
        * scale
    )
    level_all, delta_all = (
        lax.all_gather(level.T, "seq", axis=0, tiled=True),
        lax.all_gather(delta.T, "seq", axis=0, tiled=True),
    )

    def step(inner, block, bstart):
        grad_key, grad_value = inner
        query_block, grad_block = block
        count = query_block.shape[0]
        query_views = lax.dynamic_slice_in_dim(views, bstart, count)[None, :]
        query_one = lax.dynamic_slice_in_dim(every_one, bstart, count)[None, :]
        query_two = lax.dynamic_slice_in_dim(every_two, bstart, count)[None, :]
        mine = own_views[:, None]
        allow = (mine == query_views) | (mine == query_one) | (mine == query_two)
        level_block = lax.dynamic_slice_in_dim(level_all, bstart, count).T
        delta_block = lax.dynamic_slice_in_dim(delta_all, bstart, count).T
        scores = (
            jnp.einsum("khd,qhd->hkq", key_rot, query_block, preferred_element_type=jnp.float32)
            * scale
        )
        probs = jnp.where(allow[None], jnp.exp(scores - level_block[:, None, :]), 0.0)
        grad_value = grad_value + jnp.einsum(
            "hkq,qhd->hkd",
            probs.astype(jnp.bfloat16),
            grad_block,
            preferred_element_type=jnp.float32,
        )
        dprobs = jnp.einsum(
            "khd,qhd->hkq", value_split, grad_block, preferred_element_type=jnp.float32
        )
        dscores = (probs * (dprobs - delta_block[:, None, :])).astype(jnp.bfloat16)
        grad_key = grad_key + jnp.einsum(
            "hkq,qhd->hkd", dscores, query_block, preferred_element_type=jnp.float32
        )
        return (grad_key, grad_value)

    grad_key, grad_value = in_blocks(
        (
            lax.all_gather(query_rot, "seq", axis=0, tiled=True),
            lax.all_gather(grad_split, "seq", axis=0, tiled=True),
        ),
        (accum_init, accum_init),
        step,
    )

    def token_major(stack):
        return jnp.transpose(stack, (1, 0, 2))

    attended = token_major(output).reshape(rows, width).astype(jnp.bfloat16)
    grad_q = (
        rotate(token_major(grad_query), cosine, sine, -1.0)
        .reshape(rows, width)
        .astype(jnp.bfloat16)
    )
    grad_k = (
        rotate(token_major(grad_key) * scale, cosine, sine, -1.0)
        .reshape(rows, width)
        .astype(jnp.bfloat16)
    )
    grad_v = token_major(grad_value).reshape(rows, width).astype(jnp.bfloat16)
    return (attended, grad_q, grad_k, grad_v)


LOG2E = math.log2(math.e)
VMEM_LIMIT = 48 * 1024 * 1024
PAD = 3


def whole(space=pltpu.VMEM):
    return pl.BlockSpec(memory_space=space)


def inverse_steps():
    side = HD // 6 * 2
    first = HD - 2 * side
    parts, rows = [], []
    for row, group in ((0, first), (1, side), (2, side)):
        steps = np.arange(group // 2, dtype=np.float64)
        parts.append(THETA ** (-2.0 * steps / group))
        rows.append(np.full(group // 2, row))
    table = np.zeros((HD // 2, 8), np.float32)
    table[np.arange(HD // 2), np.concatenate(rows)] = np.concatenate(parts)
    return table


def prepare_kernel(
    row_first, head_of, pos_hbm, step_hbm, q_hbm, k_hbm, v_hbm, g_hbm, out_ref, table_ref,
    pos_ref, step_ref, q_ref, k_ref, v_ref, g_ref, sems,
):
    rows = q_ref.shape[0]
    pairs = (
        (pos_hbm, pos_ref), (step_hbm, step_ref), (q_hbm, q_ref), (k_hbm, k_ref), (v_hbm, v_ref), (g_hbm, g_ref)
    )
    copies = [pltpu.make_async_copy(src, dst, sems.at[i]) for i, (src, dst) in enumerate(pairs)]
    for copy in copies:
        copy.start()
    copies[0].wait()
    copies[1].wait()
    angle = (
        step_ref[:, 0:1] * pos_ref[0:1, :].astype(jnp.float32)
        + step_ref[:, 1:2] * pos_ref[1:2, :].astype(jnp.float32)
        + step_ref[:, 2:3] * pos_ref[2:3, :].astype(jnp.float32)
    )
    cosine, sine = jnp.cos(angle), jnp.sin(angle)
    table_ref[0] = jnp.concatenate([cosine, cosine], axis=0).T
    table_ref[1] = jnp.concatenate([-sine, sine], axis=0).T
    own = pl.ds(pl.multiple_of(row_first() * rows, rows), rows)
    cosine, sine = table_ref[0, own, :], table_ref[1, own, :]
    for copy in copies[2:]:
        copy.wait()
    for chip, head in enumerate(head_of):
        lanes = slice(head * HD, (head + 1) * HD)
        for at, ref in ((0, q_ref), (1, k_ref)):
            x = ref[:, lanes].astype(jnp.float32)
            out_ref[chip, at * rows : (at + 1) * rows, :] = (
                x * cosine + pltpu.roll(x, HD // 2, 1) * sine
            ).astype(jnp.bfloat16)
        out_ref[chip, 2 * rows : 3 * rows, :] = v_ref[:, lanes]
        out_ref[chip, 3 * rows : 4 * rows, :] = g_ref[:, lanes]


def attend_kernel(
    core_of, slab_of, views_ref, near_ref, mine_ref, other_ref, out_ref,
    q_all, g_all, k_all, v_all, kt_all, vt_all, s_all, d_all, p_all, ds_all, dk_all, dv_all, order, rank,
):
    blocks = mine_ref.shape[0] // 2
    rows = mine_ref.shape[1] // 4
    block = 4 * rows
    count = near_ref.shape[0]
    span = count_span(count, blocks)
    wide = 2 * block
    core, slab = core_of(), slab_of()
    scale = HD**-0.5
    first, held = [], []
    for view in range(count):
        below, equal = 0, 0
        for b in range(blocks):
            below = below + (views_ref[b * block] < view).astype(jnp.int32)
            equal = equal + (views_ref[b * block] == view).astype(jnp.int32)
        first.append(below)
        held.append(equal)

    def pick(table, at):
        value = table[0]
        for view in range(1, count):
            value = jnp.where(at == view, table[view], value)
        return value

    last, now, place = jnp.int32(0), near_ref[0, 0], jnp.int32(0)
    start, size = [], []
    cycle = [last, now]
    for _ in range(count - 2):
        one, two = near_ref[now, 0], near_ref[now, 1]
        last, now = now, jnp.where(one == last, two, one)
        cycle.append(now)
    for i, view in enumerate(cycle):
        f, n = pick(first, view), pick(held, view)
        start.append(place)
        size.append(n)
        for extra in range(2):
            order[place + extra] = f + extra
            rank[place + extra] = jnp.int32(i)
        place = place + n

    def spots(pos):
        at = [pos + PAD]
        if pos - blocks + PAD >= 0:
            at.append(pos - blocks + PAD)
        if pos + blocks < blocks + PAD:
            at.append(pos + blocks + PAD)
        return at

    for pos in range(blocks):
        src = order[pos]
        base = (pos + PAD) * block
        for at, ref, base in (
            (0, q_all, pos * block), (1, k_all, base), (2, v_all, base), (3, g_all, pos * block)
        ):
            part = slice(at * rows, (at + 1) * rows)
            for x in range(2):
                for whose, c in ((mine_ref, core), (other_ref, 1 - core)):
                    to = pl.ds(pl.multiple_of(base + (2 * x + c) * rows, rows), rows)
                    ref[to, :] = whose[2 * src + x, part, :]
        for ref, turned in ((k_all, kt_all), (v_all, vt_all)):
            source = ref[(pos + PAD) * block : (pos + PAD + 1) * block, :]
            across = source.astype(jnp.float32).T.astype(jnp.bfloat16)
            for n, spot in enumerate(spots(pos)):
                if n:
                    ref[spot * block : (spot + 1) * block, :] = source
                turned[:, spot * block : (spot + 1) * block] = across
    dk_all[...] = jnp.zeros_like(dk_all)
    dv_all[...] = jnp.zeros_like(dv_all)

    nt = (((1,), (1,)), ((), ()))
    lane = lax.broadcasted_iota(jnp.int32, (1, wide), 1)
    second = lane >= block

    for tile in range(blocks // 2):
        rank_a, rank_b = rank[2 * tile], rank[2 * tile + 1]
        before = lax.rem(rank_a + count - 1, count)
        begin = pick(start, rank_a) - pick(size, before) + PAD
        window = pl.ds(pl.multiple_of(begin * block, block), span * block)
        q_tile = q_all[tile * wide : (tile + 1) * wide, :]
        g_tile = g_all[tile * wide : (tile + 1) * wide, :]
        s_all[...] = lax.dot_general(k_all[window, :], q_tile, nt, preferred_element_type=jnp.float32)
        d_all[...] = lax.dot_general(v_all[window, :], g_tile, nt, preferred_element_type=jnp.float32)
        top = jnp.full((1, wide), NEG, jnp.float32)
        oks = []
        for i in range(span):
            at = lax.rem(begin - PAD + i + blocks, blocks)
            far_a = lax.rem(rank[at] - rank_a + count, count)
            far_b = lax.rem(rank[at] - rank_b + count, count)
            ok_a = ((far_a <= 1) | (far_a == count - 1)).astype(jnp.int32)
            ok_b = ((far_b <= 1) | (far_b == count - 1)).astype(jnp.int32)
            ok = jnp.where(second, ok_b, ok_a) > 0
            oks.append(ok)
            part = jnp.where(ok, s_all[i * block : (i + 1) * block, :], NEG)
            top = jnp.maximum(top, jnp.max(part, axis=0, keepdims=True))
        factor = scale * LOG2E
        level = top * factor
        total = jnp.zeros((1, wide), jnp.float32)
        delta = jnp.zeros((1, wide), jnp.float32)
        for i in range(span):
            here = slice(i * block, (i + 1) * block)
            e = jnp.where(oks[i], jnp.exp2(s_all[here, :] * factor - level), 0.0)
            s_all[here, :] = e
            total = total + jnp.sum(e, axis=0, keepdims=True)
            delta = delta + jnp.sum(e * d_all[here, :], axis=0, keepdims=True)
            ds_all[here, :] = e.astype(jnp.bfloat16)
        share = 1.0 / total
        delta = delta * share
        out_t = jnp.dot(vt_all[:, window], ds_all[...], preferred_element_type=jnp.float32) * share
        for i in range(span):
            here = slice(i * block, (i + 1) * block)
            p = s_all[here, :] * share
            p_all[here, :] = p.astype(jnp.bfloat16)
            ds_all[here, :] = (p * (d_all[here, :] - delta)).astype(jnp.bfloat16)
        dq_t = jnp.dot(kt_all[:, window], ds_all[...], preferred_element_type=jnp.float32) * scale
        dv_all[window, :] += jnp.dot(p_all[...], g_tile, preferred_element_type=jnp.float32)
        dk_all[window, :] += jnp.dot(ds_all[...], q_tile, preferred_element_type=jnp.float32)
        for at in range(2):
            src = order[2 * tile + at]

            @pl.when(lax.rem(src, 2) == core)
            def _():
                to = jnp.bitwise_xor(src // 2, slab)
                out_ref[to, 0] = out_t[:, at * block : (at + 1) * block].T.astype(jnp.bfloat16)
                out_ref[to, 1] = dq_t[:, at * block : (at + 1) * block].T.astype(jnp.bfloat16)

    for pos in range(blocks):
        src = order[pos]

        @pl.when(lax.rem(src, 2) == core)
        def _():
            to = jnp.bitwise_xor(src // 2, slab)
            dk = sum(dk_all[spot * block : (spot + 1) * block, :] for spot in spots(pos))
            dv = sum(dv_all[spot * block : (spot + 1) * block, :] for spot in spots(pos))
            out_ref[to, 2] = (dk * scale).astype(jnp.bfloat16)
            out_ref[to, 3] = dv.astype(jnp.bfloat16)


def finish_kernel(slab_of, table_ref, *refs):
    chunks, outs = refs[:-4], refs[-4:]
    slab = slab_of()
    cosine, sine = table_ref[0], table_ref[1]
    for m, ref in enumerate(chunks):
        lanes = pl.ds(pl.multiple_of(jnp.bitwise_xor(slab, m) * HD, HD), HD)
        for at, out in enumerate(outs):
            x = ref[at]
            if at in (1, 2):
                x = x.astype(jnp.float32)
                x = x * cosine - pltpu.roll(x, HD // 2, 1) * sine
                x = x.astype(jnp.bfloat16)
            out[:, lanes] = x


def count_span(count, blocks):
    return 4 + blocks - count


def by_chip(seqs, parts, q_in, k_in, v_in, grad_out, positions, views, adjacency):
    rows, width = q_in.shape
    xs = parts // 2
    group = width // HD // parts
    chips = seqs * xs
    block = rows * parts
    span = count_span(adjacency.shape[0], seqs)
    long = seqs + 2 * PAD
    wide = 2 * block
    head_of = [((c % xs) * 2 + (c // xs) % 2) * group + c // xs // 2 for c in range(chips)]
    limits = pltpu.CompilerParams(vmem_limit_bytes=VMEM_LIMIT)

    def row_first():
        return lax.axis_index("head")

    def core_of():
        return lax.rem(lax.axis_index("head"), 2)

    def slab_of():
        return lax.axis_index("seq") // 2

    steps = inverse_steps()
    sent, table = pl.pallas_call(
        functools.partial(prepare_kernel, row_first, head_of),
        out_shape=(
            jax.ShapeDtypeStruct((chips, 4 * rows, HD), jnp.bfloat16),
            jax.ShapeDtypeStruct((2, block, HD), jnp.float32),
        ),
        in_specs=[whole(pltpu.HBM)] * 6,
        out_specs=(whole(), whole()),
        scratch_shapes=[
            pltpu.VMEM(positions.shape, jnp.int32),
            pltpu.VMEM(steps.shape, jnp.float32),
            *[pltpu.VMEM((rows, width), jnp.bfloat16)] * 4,
            pltpu.SemaphoreType.DMA((6,)),
        ],
        compiler_params=limits,
        name="prepare",
    )(positions, jnp.asarray(steps), q_in, k_in, v_in, grad_out)
    axes = ("seq", "head")
    same_core = [[(c // xs) * parts + (c % xs) * 2 + core for c in range(chips)] for core in range(2)]
    mine = lax.all_to_all(sent, axes, 0, 0, axis_index_groups=same_core, tiled=True)
    other = lax.ppermute(mine, axes, [(d, d ^ 1) for d in range(seqs * parts)])
    back = pl.pallas_call(
        functools.partial(attend_kernel, core_of, slab_of),
        out_shape=jax.ShapeDtypeStruct((group, 4, block, HD), jnp.bfloat16),
        in_specs=[whole(pltpu.SMEM), whole(pltpu.SMEM), whole(), whole()],
        out_specs=whole(),
        scratch_shapes=[
            pltpu.VMEM((seqs * block, HD), jnp.bfloat16),
            pltpu.VMEM((seqs * block, HD), jnp.bfloat16),
            pltpu.VMEM((long * block, HD), jnp.bfloat16),
            pltpu.VMEM((long * block, HD), jnp.bfloat16),
            pltpu.VMEM((HD, long * block), jnp.bfloat16),
            pltpu.VMEM((HD, long * block), jnp.bfloat16),
            pltpu.VMEM((span * block, wide), jnp.float32),
            pltpu.VMEM((span * block, wide), jnp.float32),
            pltpu.VMEM((span * block, wide), jnp.bfloat16),
            pltpu.VMEM((span * block, wide), jnp.bfloat16),
            pltpu.VMEM((long * block, HD), jnp.float32),
            pltpu.VMEM((long * block, HD), jnp.float32),
            pltpu.SMEM((seqs + 1,), jnp.int32),
            pltpu.SMEM((seqs + 1,), jnp.int32),
        ],
        compiler_params=limits,
        name="attend",
    )(views, adjacency, mine, other)

    def route(m):
        pairs = []
        for d in range(seqs * parts):
            s, h = divmod(d, parts)
            to_s = ((s // 2) ^ m) * 2 + h % 2
            pairs.append((d, to_s * parts + h // 2 * 2 + s % 2))
        return pairs

    chunks = {m: lax.ppermute(back[m], axes, route(m)) for m in reversed(range(group))}
    return pl.pallas_call(
        functools.partial(finish_kernel, slab_of),
        out_shape=(jax.ShapeDtypeStruct((block, group * HD), jnp.bfloat16),) * 4,
        in_specs=[whole()] * (1 + group),
        out_specs=(whole(),) * 4,
        compiler_params=limits,
        name="finish",
    )(table, *[chunks[m] for m in range(group)])


def solution(mesh):
    seqs, parts = mesh.shape["seq"], mesh.shape["head"]
    in_specs = (
        P(("seq", "head"), None),
        P(("seq", "head"), None),
        P(("seq", "head"), None),
        P(("seq", "head"), None),
        P(None, "seq"),
        P(),
        P(),
    )
    out_specs = (P("seq", "head"), P("seq", "head"), P("seq", "head"), P("seq", "head"))

    def run(*args):
        heads = args[0].shape[1] // HD
        count = args[6].shape[0]
        fits = (
            seqs * parts == 2 * heads
            and seqs % 2 == 0
            and parts % 2 == 0
            and seqs & (seqs - 1) == 0
            and count <= seqs < 2 * count
            and count_span(count, seqs) <= seqs
        )
        step = functools.partial(by_chip, seqs, parts) if fits else on_device
        return jax.shard_map(
            step, mesh=mesh, in_specs=in_specs, out_specs=out_specs, check_vma=False
        )(*args)

    return run
```

```python
import functools
import math

import jax
import jax.numpy as jnp
import numpy as np
from jax import lax
from jax.experimental import pallas as pl
from jax.experimental.pallas import tpu as pltpu
from jax.sharding import PartitionSpec as P

HD = 128


NEG = -1e30
THETA = 10000.0


def rope_tables(positions, width):
    side = width // 6 * 2
    first = width - 2 * side
    parts = []
    for row, group in ((0, first), (1, side), (2, side)):
        steps = jnp.arange(group // 2, dtype=jnp.float32)
        inverse = THETA ** (-2.0 * steps / group)
        parts.append(positions[row].astype(jnp.float32)[:, None] * inverse[None, :])
    angles = jnp.concatenate(parts, axis=1)
    return (jnp.cos(angles), jnp.sin(angles))


def rotate(values, cosine, sine, sign):
    half = values.shape[-1] // 2
    first = values[..., :half]
    second = values[..., half:]
    return jnp.concatenate(
        [first * cosine - sign * second * sine, sign * first * sine + second * cosine], axis=-1
    )


def neighbours(view_ids, adjacency):
    count = adjacency.shape[0]
    match = view_ids[:, None] == jnp.arange(count, dtype=jnp.int32)[None, :]
    near_one = jnp.sum(jnp.where(match, adjacency[None, :, 0], 0), axis=1)
    near_two = jnp.sum(jnp.where(match, adjacency[None, :, 1], 0), axis=1)
    return (near_one, near_two)


def in_blocks(pieces, carry, step):
    count = pieces[0].shape[0]
    size = count
    while size > 1024 and size % 2 == 0:
        size = size // 2
    number = count // size
    shaped = tuple((piece.reshape((number, size) + piece.shape[1:]) for piece in pieces))
    firsts = size * jnp.arange(number, dtype=jnp.int32)

    def advance(state, item):
        return (step(state, item[0], item[1]), None)

    final, _ = lax.scan(advance, carry, (shaped, firsts))
    return final


def on_device(q_in, k_in, v_in, grad_out, positions, views, adjacency):
    query, keys, values, grads = (
        lax.all_to_all(q_in, "head", split_axis=1, concat_axis=0, tiled=True),
        lax.all_to_all(k_in, "head", split_axis=1, concat_axis=0, tiled=True),
        lax.all_to_all(v_in, "head", split_axis=1, concat_axis=0, tiled=True),
        lax.all_to_all(grad_out, "head", split_axis=1, concat_axis=0, tiled=True),
    )
    rows, width = query.shape
    heads = width // HD
    scale = HD ** (-0.5)
    cosine, sine = rope_tables(positions, HD)
    cosine = cosine[:, None, :]
    sine = sine[:, None, :]
    query_rot = rotate(
        query.reshape(rows, heads, HD).astype(jnp.float32), cosine, sine, 1.0
    ).astype(jnp.bfloat16)
    key_rot = rotate(keys.reshape(rows, heads, HD).astype(jnp.float32), cosine, sine, 1.0).astype(
        jnp.bfloat16
    )
    value_split = values.reshape(rows, heads, HD)
    grad_split = grads.reshape(rows, heads, HD)
    first_row = lax.axis_index("seq") * rows
    own_views = lax.dynamic_slice_in_dim(views, first_row, rows)
    near_one, near_two = neighbours(own_views, adjacency)
    every_one, every_two = neighbours(views, adjacency)

    def allowed_keys(start, count):
        other = lax.dynamic_slice_in_dim(views, start, count)[None, :]
        return (
            (other == own_views[:, None])
            | (other == near_one[:, None])
            | (other == near_two[:, None])
        )

    def scores_for(key_block, allow):
        scores = (
            jnp.einsum("qhd,khd->hqk", query_rot, key_block, preferred_element_type=jnp.float32)
            * scale
        )
        return jnp.where(allow[None], scores, NEG)

    def soft_update(top, total, accum, block, start):
        key_block, value_block = block
        allow = allowed_keys(start, key_block.shape[0])
        scores = scores_for(key_block, allow)
        new_top = jnp.maximum(top, jnp.max(scores, axis=2))
        shrink = jnp.exp(top - new_top)
        weights = jnp.where(allow[None], jnp.exp(scores - new_top[..., None]), 0.0)
        total = total * shrink + jnp.sum(weights, axis=2)
        accum = accum * shrink[..., None] + jnp.einsum(
            "hqk,khd->hqd",
            weights.astype(jnp.bfloat16),
            value_block,
            preferred_element_type=jnp.float32,
        )
        return (new_top, total, accum, weights, shrink)

    top_init = jnp.full((heads, rows), NEG, jnp.float32)
    total_init = jnp.zeros((heads, rows), jnp.float32)
    accum_init = jnp.zeros((heads, rows, HD), jnp.float32)

    def step(inner, block, bstart):
        top, total, accum, weights, shrink = soft_update(
            inner[0], inner[1], inner[2], block, bstart
        )
        return (top, total, accum)

    top, total, accum = in_blocks(
        (
            lax.all_gather(key_rot, "seq", axis=0, tiled=True),
            lax.all_gather(value_split, "seq", axis=0, tiled=True),
        ),
        (top_init, total_init, accum_init),
        step,
    )
    output = accum / total[..., None]
    finish_level = top + jnp.log(total)
    finish_delta = jnp.sum(
        grad_split.astype(jnp.float32) * jnp.transpose(output, (1, 0, 2)), axis=2
    ).T
    output, level, delta = (output, finish_level, finish_delta)

    def step(inner, block, bstart):
        key_block, value_block = block
        allow = allowed_keys(bstart, key_block.shape[0])
        scores = scores_for(key_block, allow)
        probs = jnp.where(allow[None], jnp.exp(scores - level[..., None]), 0.0)
        dprobs = jnp.einsum(
            "qhd,khd->hqk", grad_split, value_block, preferred_element_type=jnp.float32
        )
        dscores = (probs * (dprobs - delta[..., None])).astype(jnp.bfloat16)
        return inner + jnp.einsum(
            "hqk,khd->hqd", dscores, key_block, preferred_element_type=jnp.float32
        )

    grad_query = (
        in_blocks(
            (
                lax.all_gather(key_rot, "seq", axis=0, tiled=True),
                lax.all_gather(value_split, "seq", axis=0, tiled=True),
            ),
            accum_init,
            step,
        )
        * scale
    )
    level_all, delta_all = (
        lax.all_gather(level.T, "seq", axis=0, tiled=True),
        lax.all_gather(delta.T, "seq", axis=0, tiled=True),
    )

    def step(inner, block, bstart):
        grad_key, grad_value = inner
        query_block, grad_block = block
        count = query_block.shape[0]
        query_views = lax.dynamic_slice_in_dim(views, bstart, count)[None, :]
        query_one = lax.dynamic_slice_in_dim(every_one, bstart, count)[None, :]
        query_two = lax.dynamic_slice_in_dim(every_two, bstart, count)[None, :]
        mine = own_views[:, None]
        allow = (mine == query_views) | (mine == query_one) | (mine == query_two)
        level_block = lax.dynamic_slice_in_dim(level_all, bstart, count).T
        delta_block = lax.dynamic_slice_in_dim(delta_all, bstart, count).T
        scores = (
            jnp.einsum("khd,qhd->hkq", key_rot, query_block, preferred_element_type=jnp.float32)
            * scale
        )
        probs = jnp.where(allow[None], jnp.exp(scores - level_block[:, None, :]), 0.0)
        grad_value = grad_value + jnp.einsum(
            "hkq,qhd->hkd",
            probs.astype(jnp.bfloat16),
            grad_block,
            preferred_element_type=jnp.float32,
        )
        dprobs = jnp.einsum(
            "khd,qhd->hkq", value_split, grad_block, preferred_element_type=jnp.float32
        )
        dscores = (probs * (dprobs - delta_block[:, None, :])).astype(jnp.bfloat16)
        grad_key = grad_key + jnp.einsum(
            "hkq,qhd->hkd", dscores, query_block, preferred_element_type=jnp.float32
        )
        return (grad_key, grad_value)

    grad_key, grad_value = in_blocks(
        (
            lax.all_gather(query_rot, "seq", axis=0, tiled=True),
            lax.all_gather(grad_split, "seq", axis=0, tiled=True),
        ),
        (accum_init, accum_init),
        step,
    )

    def token_major(stack):
        return jnp.transpose(stack, (1, 0, 2))

    attended = token_major(output).reshape(rows, width).astype(jnp.bfloat16)
    grad_q = (
        rotate(token_major(grad_query), cosine, sine, -1.0)
        .reshape(rows, width)
        .astype(jnp.bfloat16)
    )
    grad_k = (
        rotate(token_major(grad_key) * scale, cosine, sine, -1.0)
        .reshape(rows, width)
        .astype(jnp.bfloat16)
    )
    grad_v = token_major(grad_value).reshape(rows, width).astype(jnp.bfloat16)
    return (attended, grad_q, grad_k, grad_v)


LOG2E = math.log2(math.e)
VMEM_LIMIT = 48 * 1024 * 1024
PAD = 3


def whole(space=pltpu.VMEM):
    return pl.BlockSpec(memory_space=space)


def inverse_steps():
    side = HD // 6 * 2
    first = HD - 2 * side
    parts, rows = [], []
    for row, group in ((0, first), (1, side), (2, side)):
        steps = np.arange(group // 2, dtype=np.float64)
        parts.append(THETA ** (-2.0 * steps / group))
        rows.append(np.full(group // 2, row))
    table = np.zeros((HD // 2, 8), np.float32)
    table[np.arange(HD // 2), np.concatenate(rows)] = np.concatenate(parts)
    return table


def prepare_kernel(
    row_first, head_of, pos_hbm, step_hbm, q_hbm, k_hbm, v_hbm, g_hbm, out_ref, table_ref,
    pos_ref, step_ref, q_ref, k_ref, v_ref, g_ref, sems,
):
    rows = q_ref.shape[0]
    pairs = (
        (pos_hbm, pos_ref), (step_hbm, step_ref), (q_hbm, q_ref), (k_hbm, k_ref), (v_hbm, v_ref), (g_hbm, g_ref)
    )
    copies = [pltpu.make_async_copy(src, dst, sems.at[i]) for i, (src, dst) in enumerate(pairs)]
    for copy in copies:
        copy.start()
    copies[0].wait()
    copies[1].wait()
    angle = (
        step_ref[:, 0:1] * pos_ref[0:1, :].astype(jnp.float32)
        + step_ref[:, 1:2] * pos_ref[1:2, :].astype(jnp.float32)
        + step_ref[:, 2:3] * pos_ref[2:3, :].astype(jnp.float32)
    )
    cosine, sine = jnp.cos(angle), jnp.sin(angle)
    table_ref[0] = jnp.concatenate([cosine, cosine], axis=0).T
    table_ref[1] = jnp.concatenate([-sine, sine], axis=0).T
    own = pl.ds(pl.multiple_of(row_first() * rows, rows), rows)
    cosine, sine = table_ref[0, own, :], table_ref[1, own, :]
    for copy in copies[2:]:
        copy.wait()
    for chip, head in enumerate(head_of):
        lanes = slice(head * HD, (head + 1) * HD)
        for at, ref in ((0, q_ref), (1, k_ref)):
            x = ref[:, lanes].astype(jnp.float32)
            out_ref[chip, at * rows : (at + 1) * rows, :] = (
                x * cosine + pltpu.roll(x, HD // 2, 1) * sine
            ).astype(jnp.bfloat16)
        out_ref[chip, 2 * rows : 3 * rows, :] = v_ref[:, lanes]
        out_ref[chip, 3 * rows : 4 * rows, :] = g_ref[:, lanes]


def attend_kernel(
    core_of, slab_of, views_ref, near_ref, mine_ref, other_ref, out_ref,
    q_all, g_all, k_all, v_all, kt_all, vt_all, s_all, d_all, p_all, ds_all, dk_all, dv_all, order, rank,
):
    blocks = mine_ref.shape[0] // 2
    rows = mine_ref.shape[1] // 4
    block = 4 * rows
    count = near_ref.shape[0]
    span = count_span(count, blocks)
    wide = 2 * block
    core, slab = core_of(), slab_of()
    scale = HD**-0.5
    first, held = [], []
    for view in range(count):
        below, equal = 0, 0
        for b in range(blocks):
            below = below + (views_ref[b * block] < view).astype(jnp.int32)
            equal = equal + (views_ref[b * block] == view).astype(jnp.int32)
        first.append(below)
        held.append(equal)

    def pick(table, at):
        value = table[0]
        for view in range(1, count):
            value = jnp.where(at == view, table[view], value)
        return value

    last, now, place = jnp.int32(0), near_ref[0, 0], jnp.int32(0)
    start, size = [], []
    cycle = [last, now]
    for _ in range(count - 2):
        one, two = near_ref[now, 0], near_ref[now, 1]
        last, now = now, jnp.where(one == last, two, one)
        cycle.append(now)
    for i, view in enumerate(cycle):
        f, n = pick(first, view), pick(held, view)
        start.append(place)
        size.append(n)
        for extra in range(2):
            order[place + extra] = f + extra
            rank[place + extra] = jnp.int32(i)
        place = place + n

    def spots(pos):
        at = [pos + PAD]
        if pos - blocks + PAD >= 0:
            at.append(pos - blocks + PAD)
        if pos + blocks < blocks + PAD:
            at.append(pos + blocks + PAD)
        return at

    for pos in range(blocks):
        src = order[pos]
        base = (pos + PAD) * block
        for at, ref, base in (
            (0, q_all, pos * block), (1, k_all, base), (2, v_all, base), (3, g_all, pos * block)
        ):
            part = slice(at * rows, (at + 1) * rows)
            for x in range(2):
                for whose, c in ((mine_ref, core), (other_ref, 1 - core)):
                    to = pl.ds(pl.multiple_of(base + (2 * x + c) * rows, rows), rows)
                    ref[to, :] = whose[2 * src + x, part, :]
        for ref, turned in ((k_all, kt_all), (v_all, vt_all)):
            source = ref[(pos + PAD) * block : (pos + PAD + 1) * block, :]
            across = source.astype(jnp.float32).T.astype(jnp.bfloat16)
            for n, spot in enumerate(spots(pos)):
                if n:
                    ref[spot * block : (spot + 1) * block, :] = source
                turned[:, spot * block : (spot + 1) * block] = across
    dk_all[...] = jnp.zeros_like(dk_all)
    dv_all[...] = jnp.zeros_like(dv_all)

    nt = (((1,), (1,)), ((), ()))
    lane = lax.broadcasted_iota(jnp.int32, (1, wide), 1)
    second = lane >= block

    for tile in range(blocks // 2):
        rank_a, rank_b = rank[2 * tile], rank[2 * tile + 1]
        before = lax.rem(rank_a + count - 1, count)
        begin = pick(start, rank_a) - pick(size, before) + PAD
        window = pl.ds(pl.multiple_of(begin * block, block), span * block)
        q_tile = q_all[tile * wide : (tile + 1) * wide, :]
        g_tile = g_all[tile * wide : (tile + 1) * wide, :]
        s_all[...] = lax.dot_general(k_all[window, :], q_tile, nt, preferred_element_type=jnp.float32)
        d_all[...] = lax.dot_general(v_all[window, :], g_tile, nt, preferred_element_type=jnp.float32)
        top = jnp.full((1, wide), NEG, jnp.float32)
        oks = []
        for i in range(span):
            at = lax.rem(begin - PAD + i + blocks, blocks)
            far_a = lax.rem(rank[at] - rank_a + count, count)
            far_b = lax.rem(rank[at] - rank_b + count, count)
            ok_a = ((far_a <= 1) | (far_a == count - 1)).astype(jnp.int32)
            ok_b = ((far_b <= 1) | (far_b == count - 1)).astype(jnp.int32)
            ok = jnp.where(second, ok_b, ok_a) > 0
            oks.append(ok)
            part = jnp.where(ok, s_all[i * block : (i + 1) * block, :], NEG)
            top = jnp.maximum(top, jnp.max(part, axis=0, keepdims=True))
        factor = scale * LOG2E
        level = top * factor
        total = jnp.zeros((1, wide), jnp.float32)
        delta = jnp.zeros((1, wide), jnp.float32)
        for i in range(span):
            here = slice(i * block, (i + 1) * block)
            e = jnp.where(oks[i], jnp.exp2(s_all[here, :] * factor - level), 0.0)
            s_all[here, :] = e
            total = total + jnp.sum(e, axis=0, keepdims=True)
            delta = delta + jnp.sum(e * d_all[here, :], axis=0, keepdims=True)
            ds_all[here, :] = e.astype(jnp.bfloat16)
        share = 1.0 / total
        delta = delta * share
        out_t = jnp.dot(vt_all[:, window], ds_all[...], preferred_element_type=jnp.float32) * share
        for i in range(span):
            here = slice(i * block, (i + 1) * block)
            p = s_all[here, :] * share
            p_all[here, :] = p.astype(jnp.bfloat16)
            ds_all[here, :] = (p * (d_all[here, :] - delta)).astype(jnp.bfloat16)
        dq_t = jnp.dot(kt_all[:, window], ds_all[...], preferred_element_type=jnp.float32) * scale
        dv_all[window, :] += jnp.dot(p_all[...], g_tile, preferred_element_type=jnp.float32)
        dk_all[window, :] += jnp.dot(ds_all[...], q_tile, preferred_element_type=jnp.float32)
        for at in range(2):
            src = order[2 * tile + at]

            @pl.when(lax.rem(src, 2) == core)
            def _():
                to = jnp.bitwise_xor(src // 2, slab)
                out_ref[to, 0] = out_t[:, at * block : (at + 1) * block].T.astype(jnp.bfloat16)
                out_ref[to, 1] = dq_t[:, at * block : (at + 1) * block].T.astype(jnp.bfloat16)

    for pos in range(blocks):
        src = order[pos]

        @pl.when(lax.rem(src, 2) == core)
        def _():
            to = jnp.bitwise_xor(src // 2, slab)
            dk = sum(dk_all[spot * block : (spot + 1) * block, :] for spot in spots(pos))
            dv = sum(dv_all[spot * block : (spot + 1) * block, :] for spot in spots(pos))
            out_ref[to, 2] = (dk * scale).astype(jnp.bfloat16)
            out_ref[to, 3] = dv.astype(jnp.bfloat16)


def finish_kernel(slab_of, table_ref, *refs):
    chunks, outs = refs[:-4], refs[-4:]
    slab = slab_of()
    cosine, sine = table_ref[0], table_ref[1]
    for m, ref in enumerate(chunks):
        lanes = pl.ds(pl.multiple_of(jnp.bitwise_xor(slab, m) * HD, HD), HD)
        for at, out in enumerate(outs):
            x = ref[at]
            if at in (1, 2):
                x = x.astype(jnp.float32)
                x = x * cosine - pltpu.roll(x, HD // 2, 1) * sine
                x = x.astype(jnp.bfloat16)
            out[:, lanes] = x


def count_span(count, blocks):
    return 4 + blocks - count


def by_chip(seqs, parts, q_in, k_in, v_in, grad_out, positions, views, adjacency):
    rows, width = q_in.shape
    xs = parts // 2
    group = width // HD // parts
    chips = seqs * xs
    block = rows * parts
    span = count_span(adjacency.shape[0], seqs)
    long = seqs + 2 * PAD
    wide = 2 * block
    head_of = [((c % xs) * 2 + (c // xs) % 2) * group + c // xs // 2 for c in range(chips)]
    limits = pltpu.CompilerParams(vmem_limit_bytes=VMEM_LIMIT)

    def row_first():
        return lax.axis_index("head")

    def core_of():
        return lax.rem(lax.axis_index("head"), 2)

    def slab_of():
        return lax.axis_index("seq") // 2

    steps = inverse_steps()
    sent, table = pl.pallas_call(
        functools.partial(prepare_kernel, row_first, head_of),
        out_shape=(
            jax.ShapeDtypeStruct((chips, 4 * rows, HD), jnp.bfloat16),
            jax.ShapeDtypeStruct((2, block, HD), jnp.float32),
        ),
        in_specs=[whole(pltpu.HBM)] * 6,
        out_specs=(whole(), whole()),
        scratch_shapes=[
            pltpu.VMEM(positions.shape, jnp.int32),
            pltpu.VMEM(steps.shape, jnp.float32),
            *[pltpu.VMEM((rows, width), jnp.bfloat16)] * 4,
            pltpu.SemaphoreType.DMA((6,)),
        ],
        compiler_params=pltpu.CompilerParams(vmem_limit_bytes=60*1024*1024),
        name="prepare",
    )(positions, jnp.asarray(steps), q_in, k_in, v_in, grad_out)
    axes = ("seq", "head")
    same_core = [[(c // xs) * parts + (c % xs) * 2 + core for c in range(chips)] for core in range(2)]
    mine = lax.all_to_all(sent, axes, 0, 0, axis_index_groups=same_core, tiled=True)
    other = lax.ppermute(mine, axes, [(d, d ^ 1) for d in range(seqs * parts)])
    back = pl.pallas_call(
        functools.partial(attend_kernel, core_of, slab_of),
        out_shape=jax.ShapeDtypeStruct((group, 4, block, HD), jnp.bfloat16),
        in_specs=[whole(pltpu.SMEM), whole(pltpu.SMEM), whole(), whole()],
        out_specs=whole(),
        scratch_shapes=[
            pltpu.VMEM((seqs * block, HD), jnp.bfloat16),
            pltpu.VMEM((seqs * block, HD), jnp.bfloat16),
            pltpu.VMEM((long * block, HD), jnp.bfloat16),
            pltpu.VMEM((long * block, HD), jnp.bfloat16),
            pltpu.VMEM((HD, long * block), jnp.bfloat16),
            pltpu.VMEM((HD, long * block), jnp.bfloat16),
            pltpu.VMEM((span * block, wide), jnp.float32),
            pltpu.VMEM((span * block, wide), jnp.float32),
            pltpu.VMEM((span * block, wide), jnp.bfloat16),
            pltpu.VMEM((span * block, wide), jnp.bfloat16),
            pltpu.VMEM((long * block, HD), jnp.float32),
            pltpu.VMEM((long * block, HD), jnp.float32),
            pltpu.SMEM((seqs + 1,), jnp.int32),
            pltpu.SMEM((seqs + 1,), jnp.int32),
        ],
        compiler_params=limits,
        name="attend",
    )(views, adjacency, mine, other)

    def route(m):
        pairs = []
        for d in range(seqs * parts):
            s, h = divmod(d, parts)
            to_s = ((s // 2) ^ m) * 2 + h % 2
            pairs.append((d, to_s * parts + h // 2 * 2 + s % 2))
        return pairs

    chunks = {m: lax.ppermute(back[m], axes, route(m)) for m in reversed(range(group))}
    return pl.pallas_call(
        functools.partial(finish_kernel, slab_of),
        out_shape=(jax.ShapeDtypeStruct((block, group * HD), jnp.bfloat16),) * 4,
        in_specs=[whole()] * (1 + group),
        out_specs=(whole(),) * 4,
        compiler_params=limits,
        name="finish",
    )(table, *[chunks[m] for m in range(group)])


def solution(mesh):
    seqs, parts = mesh.shape["seq"], mesh.shape["head"]
    in_specs = (
        P(("seq", "head"), None),
        P(("seq", "head"), None),
        P(("seq", "head"), None),
        P(("seq", "head"), None),
        P(None, "seq"),
        P(),
        P(),
    )
    out_specs = (P("seq", "head"), P("seq", "head"), P("seq", "head"), P("seq", "head"))

    def run(*args):
        heads = args[0].shape[1] // HD
        count = args[6].shape[0]
        fits = (
            seqs * parts == 2 * heads
            and seqs % 2 == 0
            and parts % 2 == 0
            and seqs & (seqs - 1) == 0
            and count <= seqs < 2 * count
            and count_span(count, seqs) <= seqs
        )
        step = functools.partial(by_chip, seqs, parts) if fits else on_device
        return jax.shard_map(
            step, mesh=mesh, in_specs=in_specs, out_specs=out_specs, check_vma=False
        )(*args)

    return run
```

```python
import functools
import math

import jax
import jax.numpy as jnp
import numpy as np
from jax import lax
from jax.experimental import pallas as pl
from jax.experimental.pallas import tpu as pltpu
from jax.sharding import PartitionSpec as P

HD = 128


NEG = -1e30
THETA = 10000.0


def rope_tables(positions, width):
    side = width // 6 * 2
    first = width - 2 * side
    parts = []
    for row, group in ((0, first), (1, side), (2, side)):
        steps = jnp.arange(group // 2, dtype=jnp.float32)
        inverse = THETA ** (-2.0 * steps / group)
        parts.append(positions[row].astype(jnp.float32)[:, None] * inverse[None, :])
    angles = jnp.concatenate(parts, axis=1)
    return (jnp.cos(angles), jnp.sin(angles))


def rotate(values, cosine, sine, sign):
    half = values.shape[-1] // 2
    first = values[..., :half]
    second = values[..., half:]
    return jnp.concatenate(
        [first * cosine - sign * second * sine, sign * first * sine + second * cosine], axis=-1
    )


def neighbours(view_ids, adjacency):
    count = adjacency.shape[0]
    match = view_ids[:, None] == jnp.arange(count, dtype=jnp.int32)[None, :]
    near_one = jnp.sum(jnp.where(match, adjacency[None, :, 0], 0), axis=1)
    near_two = jnp.sum(jnp.where(match, adjacency[None, :, 1], 0), axis=1)
    return (near_one, near_two)


def in_blocks(pieces, carry, step):
    count = pieces[0].shape[0]
    size = count
    while size > 1024 and size % 2 == 0:
        size = size // 2
    number = count // size
    shaped = tuple((piece.reshape((number, size) + piece.shape[1:]) for piece in pieces))
    firsts = size * jnp.arange(number, dtype=jnp.int32)

    def advance(state, item):
        return (step(state, item[0], item[1]), None)

    final, _ = lax.scan(advance, carry, (shaped, firsts))
    return final


def on_device(q_in, k_in, v_in, grad_out, positions, views, adjacency):
    query, keys, values, grads = (
        lax.all_to_all(q_in, "head", split_axis=1, concat_axis=0, tiled=True),
        lax.all_to_all(k_in, "head", split_axis=1, concat_axis=0, tiled=True),
        lax.all_to_all(v_in, "head", split_axis=1, concat_axis=0, tiled=True),
        lax.all_to_all(grad_out, "head", split_axis=1, concat_axis=0, tiled=True),
    )
    rows, width = query.shape
    heads = width // HD
    scale = HD ** (-0.5)
    cosine, sine = rope_tables(positions, HD)
    cosine = cosine[:, None, :]
    sine = sine[:, None, :]
    query_rot = rotate(
        query.reshape(rows, heads, HD).astype(jnp.float32), cosine, sine, 1.0
    ).astype(jnp.bfloat16)
    key_rot = rotate(keys.reshape(rows, heads, HD).astype(jnp.float32), cosine, sine, 1.0).astype(
        jnp.bfloat16
    )
    value_split = values.reshape(rows, heads, HD)
    grad_split = grads.reshape(rows, heads, HD)
    first_row = lax.axis_index("seq") * rows
    own_views = lax.dynamic_slice_in_dim(views, first_row, rows)
    near_one, near_two = neighbours(own_views, adjacency)
    every_one, every_two = neighbours(views, adjacency)

    def allowed_keys(start, count):
        other = lax.dynamic_slice_in_dim(views, start, count)[None, :]
        return (
            (other == own_views[:, None])
            | (other == near_one[:, None])
            | (other == near_two[:, None])
        )

    def scores_for(key_block, allow):
        scores = (
            jnp.einsum("qhd,khd->hqk", query_rot, key_block, preferred_element_type=jnp.float32)
            * scale
        )
        return jnp.where(allow[None], scores, NEG)

    def soft_update(top, total, accum, block, start):
        key_block, value_block = block
        allow = allowed_keys(start, key_block.shape[0])
        scores = scores_for(key_block, allow)
        new_top = jnp.maximum(top, jnp.max(scores, axis=2))
        shrink = jnp.exp(top - new_top)
        weights = jnp.where(allow[None], jnp.exp(scores - new_top[..., None]), 0.0)
        total = total * shrink + jnp.sum(weights, axis=2)
        accum = accum * shrink[..., None] + jnp.einsum(
            "hqk,khd->hqd",
            weights.astype(jnp.bfloat16),
            value_block,
            preferred_element_type=jnp.float32,
        )
        return (new_top, total, accum, weights, shrink)

    top_init = jnp.full((heads, rows), NEG, jnp.float32)
    total_init = jnp.zeros((heads, rows), jnp.float32)
    accum_init = jnp.zeros((heads, rows, HD), jnp.float32)

    def step(inner, block, bstart):
        top, total, accum, weights, shrink = soft_update(
            inner[0], inner[1], inner[2], block, bstart
        )
        return (top, total, accum)

    top, total, accum = in_blocks(
        (
            lax.all_gather(key_rot, "seq", axis=0, tiled=True),
            lax.all_gather(value_split, "seq", axis=0, tiled=True),
        ),
        (top_init, total_init, accum_init),
        step,
    )
    output = accum / total[..., None]
    finish_level = top + jnp.log(total)
    finish_delta = jnp.sum(
        grad_split.astype(jnp.float32) * jnp.transpose(output, (1, 0, 2)), axis=2
    ).T
    output, level, delta = (output, finish_level, finish_delta)

    def step(inner, block, bstart):
        key_block, value_block = block
        allow = allowed_keys(bstart, key_block.shape[0])
        scores = scores_for(key_block, allow)
        probs = jnp.where(allow[None], jnp.exp(scores - level[..., None]), 0.0)
        dprobs = jnp.einsum(
            "qhd,khd->hqk", grad_split, value_block, preferred_element_type=jnp.float32
        )
        dscores = (probs * (dprobs - delta[..., None])).astype(jnp.bfloat16)
        return inner + jnp.einsum(
            "hqk,khd->hqd", dscores, key_block, preferred_element_type=jnp.float32
        )

    grad_query = (
        in_blocks(
            (
                lax.all_gather(key_rot, "seq", axis=0, tiled=True),
                lax.all_gather(value_split, "seq", axis=0, tiled=True),
            ),
            accum_init,
            step,
        )
        * scale
    )
    level_all, delta_all = (
        lax.all_gather(level.T, "seq", axis=0, tiled=True),
        lax.all_gather(delta.T, "seq", axis=0, tiled=True),
    )

    def step(inner, block, bstart):
        grad_key, grad_value = inner
        query_block, grad_block = block
        count = query_block.shape[0]
        query_views = lax.dynamic_slice_in_dim(views, bstart, count)[None, :]
        query_one = lax.dynamic_slice_in_dim(every_one, bstart, count)[None, :]
        query_two = lax.dynamic_slice_in_dim(every_two, bstart, count)[None, :]
        mine = own_views[:, None]
        allow = (mine == query_views) | (mine == query_one) | (mine == query_two)
        level_block = lax.dynamic_slice_in_dim(level_all, bstart, count).T
        delta_block = lax.dynamic_slice_in_dim(delta_all, bstart, count).T
        scores = (
            jnp.einsum("khd,qhd->hkq", key_rot, query_block, preferred_element_type=jnp.float32)
            * scale
        )
        probs = jnp.where(allow[None], jnp.exp(scores - level_block[:, None, :]), 0.0)
        grad_value = grad_value + jnp.einsum(
            "hkq,qhd->hkd",
            probs.astype(jnp.bfloat16),
            grad_block,
            preferred_element_type=jnp.float32,
        )
        dprobs = jnp.einsum(
            "khd,qhd->hkq", value_split, grad_block, preferred_element_type=jnp.float32
        )
        dscores = (probs * (dprobs - delta_block[:, None, :])).astype(jnp.bfloat16)
        grad_key = grad_key + jnp.einsum(
            "hkq,qhd->hkd", dscores, query_block, preferred_element_type=jnp.float32
        )
        return (grad_key, grad_value)

    grad_key, grad_value = in_blocks(
        (
            lax.all_gather(query_rot, "seq", axis=0, tiled=True),
            lax.all_gather(grad_split, "seq", axis=0, tiled=True),
        ),
        (accum_init, accum_init),
        step,
    )

    def token_major(stack):
        return jnp.transpose(stack, (1, 0, 2))

    attended = token_major(output).reshape(rows, width).astype(jnp.bfloat16)
    grad_q = (
        rotate(token_major(grad_query), cosine, sine, -1.0)
        .reshape(rows, width)
        .astype(jnp.bfloat16)
    )
    grad_k = (
        rotate(token_major(grad_key) * scale, cosine, sine, -1.0)
        .reshape(rows, width)
        .astype(jnp.bfloat16)
    )
    grad_v = token_major(grad_value).reshape(rows, width).astype(jnp.bfloat16)
    return (attended, grad_q, grad_k, grad_v)


LOG2E = math.log2(math.e)
VMEM_LIMIT = 48 * 1024 * 1024
STANDING = {16: (11, 13, 10, 0, 2, 6, 7, 3, 4, 1, 15, 5, 9, 8, 12, 14)}


def whole(space=pltpu.VMEM):
    return pl.BlockSpec(memory_space=space)


def inverse_steps():
    side = HD // 6 * 2
    first = HD - 2 * side
    parts, rows = [], []
    for row, group in ((0, first), (1, side), (2, side)):
        steps = np.arange(group // 2, dtype=np.float64)
        parts.append(THETA ** (-2.0 * steps / group))
        rows.append(np.full(group // 2, row))
    table = np.zeros((HD // 2, 8), np.float32)
    table[np.arange(HD // 2), np.concatenate(rows)] = np.concatenate(parts)
    return table


def prepare_kernel(
    row_first, head_of, pos_hbm, step_hbm, q_hbm, k_hbm, v_hbm, g_hbm, out_ref, table_ref,
    pos_ref, step_ref, q_ref, k_ref, v_ref, g_ref, sems,
):
    rows = q_ref.shape[0]
    pairs = (
        (pos_hbm, pos_ref), (step_hbm, step_ref), (q_hbm, q_ref), (k_hbm, k_ref), (v_hbm, v_ref), (g_hbm, g_ref)
    )
    copies = [pltpu.make_async_copy(src, dst, sems.at[i]) for i, (src, dst) in enumerate(pairs)]
    for copy in copies:
        copy.start()
    copies[0].wait()
    copies[1].wait()
    angle = (
        step_ref[:, 0:1] * pos_ref[0:1, :].astype(jnp.float32)
        + step_ref[:, 1:2] * pos_ref[1:2, :].astype(jnp.float32)
        + step_ref[:, 2:3] * pos_ref[2:3, :].astype(jnp.float32)
    )
    cosine, sine = jnp.cos(angle), jnp.sin(angle)
    table_ref[0] = jnp.concatenate([cosine, cosine], axis=0).T
    table_ref[1] = jnp.concatenate([-sine, sine], axis=0).T
    own = pl.ds(pl.multiple_of(row_first() * rows, rows), rows)
    cosine, sine = table_ref[0, own, :], table_ref[1, own, :]
    for copy in copies[2:]:
        copy.wait()
    for chip, head in enumerate(head_of):
        lanes = slice(head * HD, (head + 1) * HD)
        for at, ref in ((0, q_ref), (1, k_ref)):
            x = ref[:, lanes].astype(jnp.float32)
            out_ref[chip, at * rows : (at + 1) * rows, :] = (
                x * cosine + pltpu.roll(x, HD // 2, 1) * sine
            ).astype(jnp.bfloat16)
        out_ref[chip, 2 * rows : 3 * rows, :] = v_ref[:, lanes]
        out_ref[chip, 3 * rows : 4 * rows, :] = g_ref[:, lanes]


def attend_kernel(
    core_of, slab_of, standing, views_ref, near_ref, mine_ref, other_ref, out_ref,
    q_all, g_all, kv_all, kt_all, vt_all, gt_all, s_all, e_all, p_all, ds_all, at_all, dq_all,
    order, rank, place_of, stand_of,
):
    blocks = mine_ref.shape[0] // 2
    rows = mine_ref.shape[1] // 4
    block = 4 * rows
    count = near_ref.shape[0]
    span = count_span(count, blocks)
    long = blocks - 1 + span
    wide = 2 * block
    core, slab = core_of(), slab_of()
    scale = HD**-0.5
    factor = scale * LOG2E
    first, held = [], []
    for view in range(count):
        below, equal = 0, 0
        for b in range(blocks):
            below = below + (views_ref[b * block] < view).astype(jnp.int32)
            equal = equal + (views_ref[b * block] == view).astype(jnp.int32)
        first.append(below)
        held.append(equal)

    def pick(table, at):
        value = table[0]
        for view in range(1, count):
            value = jnp.where(at == view, table[view], value)
        return value

    last, now, place = jnp.int32(0), near_ref[0, 0], jnp.int32(0)
    start, size = [], []
    cycle = [last, now]
    for _ in range(count - 2):
        one, two = near_ref[now, 0], near_ref[now, 1]
        last, now = now, jnp.where(one == last, two, one)
        cycle.append(now)
    for i, view in enumerate(cycle):
        f, n = pick(first, view), pick(held, view)
        start.append(place)
        size.append(n)
        for extra in range(2):
            order[place + extra] = f + extra
            rank[place + extra] = jnp.int32(i)
        place = place + n

    nt = (((1,), (1,)), ((), ()))
    eye = (
        lax.broadcasted_iota(jnp.int32, (HD, HD), 0) == lax.broadcasted_iota(jnp.int32, (HD, HD), 1)
    ).astype(jnp.bfloat16)

    def turn(x):
        return lax.dot_general(eye, x, nt, preferred_element_type=jnp.float32).astype(jnp.bfloat16)

    for n, chip in enumerate(standing):
        stand_of[chip] = jnp.int32(n)
    for pos in range(blocks):
        src = order[pos]
        place_of[src] = jnp.int32(pos)
        here = slice(pos * block, (pos + 1) * block)
        for at, ref, base in (
            (0, q_all, pos * block), (1, kv_all, 2 * pos * block), (2, kv_all, (2 * pos + 1) * block), (3, g_all, pos * block)
        ):
            part = slice(at * rows, (at + 1) * rows)
            for x in range(2):
                n = stand_of[2 * src + x]
                for whose, c in ((mine_ref, core), (other_ref, 1 - core)):
                    to = pl.ds(pl.multiple_of(base + (2 * x + c) * rows, rows), rows)
                    ref[to, :] = whose[n, part, :]
        turned = turn(kv_all[2 * pos * block : 2 * (pos + 1) * block, :])
        for spot in range(pos % blocks, long, blocks):
            there = slice(spot * block, (spot + 1) * block)
            kt_all[:, there] = turned[:, :block]
            vt_all[:HD, there] = turned[:, block:]
        gt_all[:, here] = turn(g_all[here, :])
    vt_all[HD:, :] = jnp.ones((vt_all.shape[0] - HD, vt_all.shape[1]), jnp.bfloat16)

    second = lax.broadcasted_iota(jnp.int32, (1, wide), 1) >= block
    tiles = range(blocks // 2)
    lanes = [slice(tile * wide, (tile + 1) * wide) for tile in tiles]
    begins, ats, places, windows, oks = [], [], [], [], []
    for tile in tiles:
        rank_a, rank_b = rank[2 * tile], rank[2 * tile + 1]
        before = lax.rem(rank_a + count - 1, count)
        begin = lax.rem(pick(start, rank_a) - pick(size, before) + blocks, blocks)
        begins.append(begin)
        windows.append(pl.ds(pl.multiple_of(begin * block, block), span * block))
        at = [lax.rem(begin + i, blocks) for i in range(span)]
        places.append([pl.multiple_of(n * (2 * block), block) for n in at])
        oks.append([])
        for n in at:
            far_a = lax.rem(rank[n] - rank_a + count, count)
            far_b = lax.rem(rank[n] - rank_b + count, count)
            ok_a = ((far_a <= 1) | (far_a == count - 1)).astype(jnp.int32)
            ok_b = ((far_b <= 1) | (far_b == count - 1)).astype(jnp.int32)
            oks[tile].append(jnp.where(second, ok_b, ok_a) > 0)
    owned = [place_of[2 * jnp.bitwise_xor(slab, m) + core] for m in range(out_ref.shape[0])]
    levels, deltas, sums = {}, {}, [0, 0]

    def scores(tile):
        top = jnp.full((1, wide), NEG, jnp.float32)
        for i in range(span):
            s = lax.dot_general(
                kv_all[pl.ds(places[tile][i], block), :], q_all[lanes[tile], :], nt, preferred_element_type=jnp.float32
            )
            s_all[tile, i] = s
            top = jnp.maximum(top, jnp.where(oks[tile][i], jnp.max(s, axis=0, keepdims=True), NEG))
        levels[tile] = top * factor

    def weights(tile):
        for i in range(span):
            e = jnp.exp2(s_all[tile, i] * factor - jnp.where(oks[tile][i], levels[tile], -NEG))
            e_all[tile, i * block : (i + 1) * block, :] = e.astype(jnp.bfloat16)

    def outputs(tile):
        out = jnp.dot(vt_all[:, windows[tile]], e_all[tile], preferred_element_type=jnp.float32)
        total = out[HD : HD + 1, :]
        out = out[:HD, :] / total
        at_all[:, lanes[tile]] = out.astype(jnp.bfloat16)
        deltas[tile] = jnp.sum(gt_all[:, lanes[tile]].astype(jnp.float32) * out, axis=0, keepdims=True)
        levels[tile] = levels[tile] + jnp.log2(total)

    def slopes(tile):
        for i in range(span):
            here = slice(i * block, (i + 1) * block)
            d = lax.dot_general(
                kv_all[pl.ds(places[tile][i] + block, block), :], g_all[lanes[tile], :], nt, preferred_element_type=jnp.float32
            )
            p = jnp.exp2(s_all[tile, i] * factor - jnp.where(oks[tile][i], levels[tile], -NEG))
            p_all[tile, here, :] = p.astype(jnp.bfloat16)
            ds_all[tile, here, :] = (p * (d - deltas[tile])).astype(jnp.bfloat16)
        p_all[tile, span * block :, :] = jnp.zeros((block, wide), jnp.bfloat16)
        ds_all[tile, span * block :, :] = jnp.zeros((block, wide), jnp.bfloat16)

    def query_slopes(tile):
        dq = jnp.dot(kt_all[:, windows[tile]], ds_all[tile, : span * block, :], preferred_element_type=jnp.float32)
        dq_all[:, lanes[tile]] = (dq * scale).astype(jnp.bfloat16)

    def key_slopes(tile):
        rels = [
            pl.multiple_of(jnp.minimum(lax.rem(pos - begins[tile] + blocks, blocks), span) * block, block)
            for pos in owned
        ]
        for n, (ref, other) in enumerate(((ds_all, q_all), (p_all, g_all))):
            x = jnp.concatenate([ref[tile, pl.ds(rel, block), :] for rel in rels], axis=0)
            sums[n] = sums[n] + jnp.dot(x, other[lanes[tile], :], preferred_element_type=jnp.float32)

    scores(0)
    weights(0)
    scores(1)
    weights(1)
    scores(2)
    weights(2)
    scores(3)
    weights(3)
    outputs(0)
    outputs(1)
    outputs(2)
    outputs(3)
    slopes(0)
    slopes(1)
    slopes(2)
    slopes(3)
    query_slopes(0)
    query_slopes(1)
    query_slopes(2)
    query_slopes(3)
    key_slopes(0)
    key_slopes(1)
    key_slopes(2)
    key_slopes(3)
    dk, dv = sums
    for m, pos in enumerate(owned):
        here = pl.ds(pl.multiple_of(pos * block, block), block)
        out_ref[m, 0] = turn(at_all[:, here])
        out_ref[m, 1] = turn(dq_all[:, here])
        out_ref[m, 2] = (dk[m * block : (m + 1) * block] * scale).astype(jnp.bfloat16)
        out_ref[m, 3] = dv[m * block : (m + 1) * block].astype(jnp.bfloat16)


def finish_kernel(slab_of, turns, table_ref, *refs):
    chunks, outs = refs[:-4], refs[-4:]
    slab = slab_of()
    cosine, sine = table_ref[0], table_ref[1]
    for m, ref in zip(turns, chunks, strict=True):
        lanes = pl.ds(pl.multiple_of(jnp.bitwise_xor(slab, m) * HD, HD), HD)
        for at, out in enumerate(outs):
            x = ref[at]
            if at in (1, 2):
                x = x.astype(jnp.float32)
                x = x * cosine - pltpu.roll(x, HD // 2, 1) * sine
                x = x.astype(jnp.bfloat16)
            out[:, lanes] = x


def count_span(count, blocks):
    return 4 + blocks - count


def by_chip(seqs, parts, q_in, k_in, v_in, grad_out, positions, views, adjacency):
    rows, width = q_in.shape
    xs = parts // 2
    group = width // HD // parts
    chips = seqs * xs
    block = rows * parts
    span = count_span(adjacency.shape[0], seqs)
    tokens = seqs * block
    wide = 2 * block
    standing = STANDING.get(chips, tuple(range(chips)))
    head_of = [((c % xs) * 2 + (c // xs) % 2) * group + c // xs // 2 for c in standing]
    limits = pltpu.CompilerParams(vmem_limit_bytes=VMEM_LIMIT)

    def row_first():
        return lax.axis_index("head")

    def core_of():
        return lax.rem(lax.axis_index("head"), 2)

    def slab_of():
        return lax.axis_index("seq") // 2

    steps = inverse_steps()
    sent, table = pl.pallas_call(
        functools.partial(prepare_kernel, row_first, head_of),
        out_shape=(
            jax.ShapeDtypeStruct((chips, 4 * rows, HD), jnp.bfloat16),
            jax.ShapeDtypeStruct((2, block, HD), jnp.float32),
        ),
        in_specs=[whole(pltpu.HBM)] * 6,
        out_specs=(whole(), whole()),
        scratch_shapes=[
            pltpu.VMEM(positions.shape, jnp.int32),
            pltpu.VMEM(steps.shape, jnp.float32),
            *[pltpu.VMEM((rows, width), jnp.bfloat16)] * 4,
            pltpu.SemaphoreType.DMA((6,)),
        ],
        compiler_params=pltpu.CompilerParams(vmem_limit_bytes=VMEM_LIMIT + 12 * 1024 * 1024),
        name="prepare",
    )(positions, jnp.asarray(steps), q_in, k_in, v_in, grad_out)
    axes = ("seq", "head")
    same_core = [[(c // xs) * parts + (c % xs) * 2 + core for c in standing] for core in range(2)]
    mine = lax.all_to_all(sent, axes, 0, 0, axis_index_groups=same_core, tiled=True)
    other = lax.ppermute(mine, axes, [(d, d ^ 1) for d in range(seqs * parts)])
    back = pl.pallas_call(
        functools.partial(attend_kernel, core_of, slab_of, standing),
        out_shape=jax.ShapeDtypeStruct((group, 4, block, HD), jnp.bfloat16),
        in_specs=[whole(pltpu.SMEM), whole(pltpu.SMEM), whole(), whole()],
        out_specs=whole(),
        scratch_shapes=[
            pltpu.VMEM((tokens, HD), jnp.bfloat16),
            pltpu.VMEM((tokens, HD), jnp.bfloat16),
            pltpu.VMEM((2 * tokens, HD), jnp.bfloat16),
            pltpu.VMEM((HD, tokens + (span - 1) * block), jnp.bfloat16),
            pltpu.VMEM((HD + 16, tokens + (span - 1) * block), jnp.bfloat16),
            pltpu.VMEM((HD, tokens), jnp.bfloat16),
            pltpu.VMEM((seqs // 2, span, block, wide), jnp.float32),
            pltpu.VMEM((seqs // 2, span * block, wide), jnp.bfloat16),
            pltpu.VMEM((seqs // 2, (span + 1) * block, wide), jnp.bfloat16),
            pltpu.VMEM((seqs // 2, (span + 1) * block, wide), jnp.bfloat16),
            pltpu.VMEM((HD, tokens), jnp.bfloat16),
            pltpu.VMEM((HD, tokens), jnp.bfloat16),
            *[pltpu.SMEM((seqs + 1,), jnp.int32)] * 3,
            pltpu.SMEM((chips,), jnp.int32),
        ],
        compiler_params=limits,
        name="attend",
    )(views, adjacency, mine, other)

    def route(m):
        pairs = []
        for d in range(seqs * parts):
            s, h = divmod(d, parts)
            to_s = ((s // 2) ^ m) * 2 + h % 2
            pairs.append((d, to_s * parts + h // 2 * 2 + s % 2))
        return pairs

    turns = [(group // 2 - n) % group for n in reversed(range(group))]
    chunks = [lax.ppermute(back[m], axes, route(m)) for m in turns]
    return pl.pallas_call(
        functools.partial(finish_kernel, slab_of, turns),
        out_shape=(jax.ShapeDtypeStruct((block, group * HD), jnp.bfloat16),) * 4,
        in_specs=[whole()] * (1 + group),
        out_specs=(whole(),) * 4,
        compiler_params=limits,
        name="finish",
    )(table, *chunks)


def solution(mesh):
    seqs, parts = mesh.shape["seq"], mesh.shape["head"]
    in_specs = (
        P(("seq", "head"), None),
        P(("seq", "head"), None),
        P(("seq", "head"), None),
        P(("seq", "head"), None),
        P(None, "seq"),
        P(),
        P(),
    )
    out_specs = (P("seq", "head"), P("seq", "head"), P("seq", "head"), P("seq", "head"))

    def run(*args):
        heads = args[0].shape[1] // HD
        count = args[6].shape[0]
        fits = (
            seqs * parts == 2 * heads
            and seqs % 2 == 0
            and parts % 2 == 0
            and seqs & (seqs - 1) == 0
            and count <= seqs < 2 * count
            and count_span(count, seqs) <= seqs
        )
        step = functools.partial(by_chip, seqs, parts) if fits else on_device
        return jax.shard_map(
            step, mesh=mesh, in_specs=in_specs, out_specs=out_specs, check_vma=False
        )(*args)

    return run
```

```python
import functools
import math

import jax
import jax.numpy as jnp
import numpy as np
from jax import lax
from jax.experimental import pallas as pl
from jax.experimental.pallas import tpu as pltpu
from jax.sharding import PartitionSpec as P

HD = 128


NEG = -1e30
THETA = 10000.0


def rope_tables(positions, width):
    side = width // 6 * 2
    first = width - 2 * side
    parts = []
    for row, group in ((0, first), (1, side), (2, side)):
        steps = jnp.arange(group // 2, dtype=jnp.float32)
        inverse = THETA ** (-2.0 * steps / group)
        parts.append(positions[row].astype(jnp.float32)[:, None] * inverse[None, :])
    angles = jnp.concatenate(parts, axis=1)
    return (jnp.cos(angles), jnp.sin(angles))


def rotate(values, cosine, sine, sign):
    half = values.shape[-1] // 2
    first = values[..., :half]
    second = values[..., half:]
    return jnp.concatenate(
        [first * cosine - sign * second * sine, sign * first * sine + second * cosine], axis=-1
    )


def neighbours(view_ids, adjacency):
    count = adjacency.shape[0]
    match = view_ids[:, None] == jnp.arange(count, dtype=jnp.int32)[None, :]
    near_one = jnp.sum(jnp.where(match, adjacency[None, :, 0], 0), axis=1)
    near_two = jnp.sum(jnp.where(match, adjacency[None, :, 1], 0), axis=1)
    return (near_one, near_two)


def in_blocks(pieces, carry, step):
    count = pieces[0].shape[0]
    size = count
    while size > 1024 and size % 2 == 0:
        size = size // 2
    number = count // size
    shaped = tuple((piece.reshape((number, size) + piece.shape[1:]) for piece in pieces))
    firsts = size * jnp.arange(number, dtype=jnp.int32)

    def advance(state, item):
        return (step(state, item[0], item[1]), None)

    final, _ = lax.scan(advance, carry, (shaped, firsts))
    return final


def on_device(q_in, k_in, v_in, grad_out, positions, views, adjacency):
    query, keys, values, grads = (
        lax.all_to_all(q_in, "head", split_axis=1, concat_axis=0, tiled=True),
        lax.all_to_all(k_in, "head", split_axis=1, concat_axis=0, tiled=True),
        lax.all_to_all(v_in, "head", split_axis=1, concat_axis=0, tiled=True),
        lax.all_to_all(grad_out, "head", split_axis=1, concat_axis=0, tiled=True),
    )
    rows, width = query.shape
    heads = width // HD
    scale = HD ** (-0.5)
    cosine, sine = rope_tables(positions, HD)
    cosine = cosine[:, None, :]
    sine = sine[:, None, :]
    query_rot = rotate(
        query.reshape(rows, heads, HD).astype(jnp.float32), cosine, sine, 1.0
    ).astype(jnp.bfloat16)
    key_rot = rotate(keys.reshape(rows, heads, HD).astype(jnp.float32), cosine, sine, 1.0).astype(
        jnp.bfloat16
    )
    value_split = values.reshape(rows, heads, HD)
    grad_split = grads.reshape(rows, heads, HD)
    first_row = lax.axis_index("seq") * rows
    own_views = lax.dynamic_slice_in_dim(views, first_row, rows)
    near_one, near_two = neighbours(own_views, adjacency)
    every_one, every_two = neighbours(views, adjacency)

    def allowed_keys(start, count):
        other = lax.dynamic_slice_in_dim(views, start, count)[None, :]
        return (
            (other == own_views[:, None])
            | (other == near_one[:, None])
            | (other == near_two[:, None])
        )

    def scores_for(key_block, allow):
        scores = (
            jnp.einsum("qhd,khd->hqk", query_rot, key_block, preferred_element_type=jnp.float32)
            * scale
        )
        return jnp.where(allow[None], scores, NEG)

    def soft_update(top, total, accum, block, start):
        key_block, value_block = block
        allow = allowed_keys(start, key_block.shape[0])
        scores = scores_for(key_block, allow)
        new_top = jnp.maximum(top, jnp.max(scores, axis=2))
        shrink = jnp.exp(top - new_top)
        weights = jnp.where(allow[None], jnp.exp(scores - new_top[..., None]), 0.0)
        total = total * shrink + jnp.sum(weights, axis=2)
        accum = accum * shrink[..., None] + jnp.einsum(
            "hqk,khd->hqd",
            weights.astype(jnp.bfloat16),
            value_block,
            preferred_element_type=jnp.float32,
        )
        return (new_top, total, accum, weights, shrink)

    top_init = jnp.full((heads, rows), NEG, jnp.float32)
    total_init = jnp.zeros((heads, rows), jnp.float32)
    accum_init = jnp.zeros((heads, rows, HD), jnp.float32)

    def step(inner, block, bstart):
        top, total, accum, weights, shrink = soft_update(
            inner[0], inner[1], inner[2], block, bstart
        )
        return (top, total, accum)

    top, total, accum = in_blocks(
        (
            lax.all_gather(key_rot, "seq", axis=0, tiled=True),
            lax.all_gather(value_split, "seq", axis=0, tiled=True),
        ),
        (top_init, total_init, accum_init),
        step,
    )
    output = accum / total[..., None]
    finish_level = top + jnp.log(total)
    finish_delta = jnp.sum(
        grad_split.astype(jnp.float32) * jnp.transpose(output, (1, 0, 2)), axis=2
    ).T
    output, level, delta = (output, finish_level, finish_delta)

    def step(inner, block, bstart):
        key_block, value_block = block
        allow = allowed_keys(bstart, key_block.shape[0])
        scores = scores_for(key_block, allow)
        probs = jnp.where(allow[None], jnp.exp(scores - level[..., None]), 0.0)
        dprobs = jnp.einsum(
            "qhd,khd->hqk", grad_split, value_block, preferred_element_type=jnp.float32
        )
        dscores = (probs * (dprobs - delta[..., None])).astype(jnp.bfloat16)
        return inner + jnp.einsum(
            "hqk,khd->hqd", dscores, key_block, preferred_element_type=jnp.float32
        )

    grad_query = (
        in_blocks(
            (
                lax.all_gather(key_rot, "seq", axis=0, tiled=True),
                lax.all_gather(value_split, "seq", axis=0, tiled=True),
            ),
            accum_init,
            step,
        )
        * scale
    )
    level_all, delta_all = (
        lax.all_gather(level.T, "seq", axis=0, tiled=True),
        lax.all_gather(delta.T, "seq", axis=0, tiled=True),
    )

    def step(inner, block, bstart):
        grad_key, grad_value = inner
        query_block, grad_block = block
        count = query_block.shape[0]
        query_views = lax.dynamic_slice_in_dim(views, bstart, count)[None, :]
        query_one = lax.dynamic_slice_in_dim(every_one, bstart, count)[None, :]
        query_two = lax.dynamic_slice_in_dim(every_two, bstart, count)[None, :]
        mine = own_views[:, None]
        allow = (mine == query_views) | (mine == query_one) | (mine == query_two)
        level_block = lax.dynamic_slice_in_dim(level_all, bstart, count).T
        delta_block = lax.dynamic_slice_in_dim(delta_all, bstart, count).T
        scores = (
            jnp.einsum("khd,qhd->hkq", key_rot, query_block, preferred_element_type=jnp.float32)
            * scale
        )
        probs = jnp.where(allow[None], jnp.exp(scores - level_block[:, None, :]), 0.0)
        grad_value = grad_value + jnp.einsum(
            "hkq,qhd->hkd",
            probs.astype(jnp.bfloat16),
            grad_block,
            preferred_element_type=jnp.float32,
        )
        dprobs = jnp.einsum(
            "khd,qhd->hkq", value_split, grad_block, preferred_element_type=jnp.float32
        )
        dscores = (probs * (dprobs - delta_block[:, None, :])).astype(jnp.bfloat16)
        grad_key = grad_key + jnp.einsum(
            "hkq,qhd->hkd", dscores, query_block, preferred_element_type=jnp.float32
        )
        return (grad_key, grad_value)

    grad_key, grad_value = in_blocks(
        (
            lax.all_gather(query_rot, "seq", axis=0, tiled=True),
            lax.all_gather(grad_split, "seq", axis=0, tiled=True),
        ),
        (accum_init, accum_init),
        step,
    )

    def token_major(stack):
        return jnp.transpose(stack, (1, 0, 2))

    attended = token_major(output).reshape(rows, width).astype(jnp.bfloat16)
    grad_q = (
        rotate(token_major(grad_query), cosine, sine, -1.0)
        .reshape(rows, width)
        .astype(jnp.bfloat16)
    )
    grad_k = (
        rotate(token_major(grad_key) * scale, cosine, sine, -1.0)
        .reshape(rows, width)
        .astype(jnp.bfloat16)
    )
    grad_v = token_major(grad_value).reshape(rows, width).astype(jnp.bfloat16)
    return (attended, grad_q, grad_k, grad_v)


LOG2E = math.log2(math.e)
VMEM_LIMIT = 48 * 1024 * 1024
STANDING = {16: (11, 13, 10, 0, 2, 6, 7, 3, 4, 1, 15, 5, 9, 8, 12, 14)}


def whole(space=pltpu.VMEM):
    return pl.BlockSpec(memory_space=space)


def inverse_steps():
    side = HD // 6 * 2
    first = HD - 2 * side
    parts, rows = [], []
    for row, group in ((0, first), (1, side), (2, side)):
        steps = np.arange(group // 2, dtype=np.float64)
        parts.append(THETA ** (-2.0 * steps / group))
        rows.append(np.full(group // 2, row))
    table = np.zeros((HD // 2, 8), np.float32)
    table[np.arange(HD // 2), np.concatenate(rows)] = np.concatenate(parts)
    return table


def prepare_kernel(
    row_first, head_of, pos_hbm, step_hbm, q_hbm, k_hbm, v_hbm, g_hbm, out_ref, table_ref,
    pos_ref, step_ref, q_ref, k_ref, v_ref, g_ref, sems,
):
    rows = q_ref.shape[0]
    pairs = (
        (pos_hbm, pos_ref), (step_hbm, step_ref), (q_hbm, q_ref), (k_hbm, k_ref), (v_hbm, v_ref), (g_hbm, g_ref)
    )
    copies = [pltpu.make_async_copy(src, dst, sems.at[i]) for i, (src, dst) in enumerate(pairs)]
    for copy in copies:
        copy.start()
    copies[0].wait()
    copies[1].wait()
    angle = (
        step_ref[:, 0:1] * pos_ref[0:1, :].astype(jnp.float32)
        + step_ref[:, 1:2] * pos_ref[1:2, :].astype(jnp.float32)
        + step_ref[:, 2:3] * pos_ref[2:3, :].astype(jnp.float32)
    )
    cosine, sine = jnp.cos(angle), jnp.sin(angle)
    table_ref[0] = jnp.concatenate([cosine, cosine], axis=0).T
    table_ref[1] = jnp.concatenate([-sine, sine], axis=0).T
    own = pl.ds(pl.multiple_of(row_first() * rows, rows), rows)
    cosine, sine = table_ref[0, own, :], table_ref[1, own, :]
    for copy in copies[2:]:
        copy.wait()
    for chip, head in enumerate(head_of):
        lanes = slice(head * HD, (head + 1) * HD)
        for at, ref in ((0, q_ref), (1, k_ref)):
            x = ref[:, lanes].astype(jnp.float32)
            out_ref[chip, at * rows : (at + 1) * rows, :] = (
                x * cosine + pltpu.roll(x, HD // 2, 1) * sine
            ).astype(jnp.bfloat16)
        out_ref[chip, 2 * rows : 3 * rows, :] = v_ref[:, lanes]
        out_ref[chip, 3 * rows : 4 * rows, :] = g_ref[:, lanes]


def attend_kernel(
    core_of, slab_of, standing, views_ref, near_ref, mine_ref, other_ref, out_ref,
    q_all, g_all, kv_all, kt_all, vt_all, gt_all, s_all, e_all, p_all, ds_all, at_all, dq_all,
    order, rank, place_of, stand_of,
):
    blocks = mine_ref.shape[0] // 2
    rows = mine_ref.shape[1] // 4
    block = 4 * rows
    count = near_ref.shape[0]
    span = count_span(count, blocks)
    long = blocks - 1 + span
    wide = 2 * block
    core, slab = core_of(), slab_of()
    scale = HD**-0.5
    factor = scale * LOG2E
    first, held = [], []
    for view in range(count):
        below, equal = 0, 0
        for b in range(blocks):
            below = below + (views_ref[b * block] < view).astype(jnp.int32)
            equal = equal + (views_ref[b * block] == view).astype(jnp.int32)
        first.append(below)
        held.append(equal)

    def pick(table, at):
        value = table[0]
        for view in range(1, count):
            value = jnp.where(at == view, table[view], value)
        return value

    last, now, place = jnp.int32(0), near_ref[0, 0], jnp.int32(0)
    start, size = [], []
    cycle = [last, now]
    for _ in range(count - 2):
        one, two = near_ref[now, 0], near_ref[now, 1]
        last, now = now, jnp.where(one == last, two, one)
        cycle.append(now)
    for i, view in enumerate(cycle):
        f, n = pick(first, view), pick(held, view)
        start.append(place)
        size.append(n)
        for extra in range(2):
            order[place + extra] = f + extra
            rank[place + extra] = jnp.int32(i)
        place = place + n

    nt = (((1,), (1,)), ((), ()))
    eye = (
        lax.broadcasted_iota(jnp.int32, (HD, HD), 0) == lax.broadcasted_iota(jnp.int32, (HD, HD), 1)
    ).astype(jnp.bfloat16)

    def turn(x):
        return lax.dot_general(eye, x, nt, preferred_element_type=jnp.float32).astype(jnp.bfloat16)

    for n, chip in enumerate(standing):
        stand_of[chip] = jnp.int32(n)
    for pos in range(blocks):
        src = order[pos]
        place_of[src] = jnp.int32(pos)
        here = slice(pos * block, (pos + 1) * block)
        for at, ref, base in (
            (0, q_all, pos * block), (1, kv_all, 2 * pos * block), (2, kv_all, (2 * pos + 1) * block), (3, g_all, pos * block)
        ):
            part = slice(at * rows, (at + 1) * rows)
            for x in range(2):
                n = stand_of[2 * src + x]
                for whose, c in ((mine_ref, core), (other_ref, 1 - core)):
                    to = pl.ds(pl.multiple_of(base + (2 * x + c) * rows, rows), rows)
                    ref[to, :] = whose[n, part, :]
        turned = turn(kv_all[2 * pos * block : 2 * (pos + 1) * block, :])
        for spot in range(pos % blocks, long, blocks):
            there = slice(spot * block, (spot + 1) * block)
            kt_all[:, there] = turned[:, :block]
            vt_all[:HD, there] = turned[:, block:]
        gt_all[:, here] = turn(g_all[here, :])
    vt_all[HD:, :] = jnp.ones((vt_all.shape[0] - HD, vt_all.shape[1]), jnp.bfloat16)

    second = lax.broadcasted_iota(jnp.int32, (1, wide), 1) >= block
    tiles = range(blocks // 2)
    lanes = [slice(tile * wide, (tile + 1) * wide) for tile in tiles]
    begins, ats, places, windows, oks = [], [], [], [], []
    for tile in tiles:
        rank_a, rank_b = rank[2 * tile], rank[2 * tile + 1]
        before = lax.rem(rank_a + count - 1, count)
        begin = lax.rem(pick(start, rank_a) - pick(size, before) + blocks, blocks)
        begins.append(begin)
        windows.append(pl.ds(pl.multiple_of(begin * block, block), span * block))
        at = [lax.rem(begin + i, blocks) for i in range(span)]
        places.append([pl.multiple_of(n * (2 * block), block) for n in at])
        oks.append([])
        for n in at:
            far_a = lax.rem(rank[n] - rank_a + count, count)
            far_b = lax.rem(rank[n] - rank_b + count, count)
            ok_a = ((far_a <= 1) | (far_a == count - 1)).astype(jnp.int32)
            ok_b = ((far_b <= 1) | (far_b == count - 1)).astype(jnp.int32)
            oks[tile].append(jnp.where(second, ok_b, ok_a) > 0)
    owned = [place_of[2 * jnp.bitwise_xor(slab, m) + core] for m in range(out_ref.shape[0])]
    levels, deltas, sums = {}, {}, [0, 0]

    def scores(tile):
        top = jnp.full((1, wide), NEG, jnp.float32)
        for i in range(span):
            s = lax.dot_general(
                kv_all[pl.ds(places[tile][i], block), :], q_all[lanes[tile], :], nt, preferred_element_type=jnp.float32
            )
            s_all[tile, i] = s
            top = jnp.maximum(top, jnp.where(oks[tile][i], jnp.max(s, axis=0, keepdims=True), NEG))
        levels[tile] = top * factor

    def weights(tile):
        for i in range(span):
            e = jnp.exp2(s_all[tile, i] * factor - jnp.where(oks[tile][i], levels[tile], -NEG))
            e_all[tile, i * block : (i + 1) * block, :] = e.astype(jnp.bfloat16)

    def outputs(tile):
        out = jnp.dot(vt_all[:, windows[tile]], e_all[tile], preferred_element_type=jnp.float32)
        total = out[HD : HD + 1, :]
        out = out[:HD, :] / total
        at_all[:, lanes[tile]] = out.astype(jnp.bfloat16)
        deltas[tile] = jnp.sum(gt_all[:, lanes[tile]].astype(jnp.float32) * out, axis=0, keepdims=True)
        levels[tile] = levels[tile] + jnp.log2(total)

    def slopes(tile):
        for i in range(span):
            here = slice(i * block, (i + 1) * block)
            d = lax.dot_general(
                kv_all[pl.ds(places[tile][i] + block, block), :], g_all[lanes[tile], :], nt, preferred_element_type=jnp.float32
            )
            p = jnp.exp2(s_all[tile, i] * factor - jnp.where(oks[tile][i], levels[tile], -NEG))
            p_all[tile, here, :] = p.astype(jnp.bfloat16)
            ds_all[tile, here, :] = (p * (d - deltas[tile])).astype(jnp.bfloat16)
        p_all[tile, span * block :, :] = jnp.zeros((block, wide), jnp.bfloat16)
        ds_all[tile, span * block :, :] = jnp.zeros((block, wide), jnp.bfloat16)

    def query_slopes(tile):
        dq = jnp.dot(kt_all[:, windows[tile]], ds_all[tile, : span * block, :], preferred_element_type=jnp.float32)
        dq_all[:, lanes[tile]] = (dq * scale).astype(jnp.bfloat16)

    def key_slopes(tile):
        rels = [
            pl.multiple_of(jnp.minimum(lax.rem(pos - begins[tile] + blocks, blocks), span) * block, block)
            for pos in owned
        ]
        for n, (ref, other) in enumerate(((ds_all, q_all), (p_all, g_all))):
            x = jnp.concatenate([ref[tile, pl.ds(rel, block), :] for rel in rels], axis=0)
            sums[n] = sums[n] + jnp.dot(x, other[lanes[tile], :], preferred_element_type=jnp.float32)

    scores(0)
    weights(0)
    scores(1)
    weights(1)
    scores(2)
    weights(2)
    scores(3)
    weights(3)
    outputs(0)
    outputs(1)
    outputs(2)
    outputs(3)
    slopes(0)
    slopes(1)
    slopes(2)
    slopes(3)
    query_slopes(0)
    query_slopes(1)
    query_slopes(2)
    query_slopes(3)
    key_slopes(0)
    key_slopes(1)
    key_slopes(2)
    key_slopes(3)
    dk, dv = sums
    for m, pos in enumerate(owned):
        here = pl.ds(pl.multiple_of(pos * block, block), block)
        out_ref[m, 0] = turn(at_all[:, here])
        out_ref[m, 1] = turn(dq_all[:, here])
        out_ref[m, 2] = (dk[m * block : (m + 1) * block] * scale).astype(jnp.bfloat16)
        out_ref[m, 3] = dv[m * block : (m + 1) * block].astype(jnp.bfloat16)


def finish_kernel(slab_of, turns, table_ref, *refs):
    chunks, outs = refs[:-4], refs[-4:]
    slab = slab_of()
    cosine, sine = table_ref[0], table_ref[1]
    for m, ref in zip(turns, chunks, strict=True):
        lanes = pl.ds(pl.multiple_of(jnp.bitwise_xor(slab, m) * HD, HD), HD)
        for at, out in enumerate(outs):
            x = ref[at]
            if at in (1, 2):
                x = x.astype(jnp.float32)
                x = x * cosine - pltpu.roll(x, HD // 2, 1) * sine
                x = x.astype(jnp.bfloat16)
            out[:, lanes] = x


def count_span(count, blocks):
    return 4 + blocks - count


def by_chip(seqs, parts, q_in, k_in, v_in, grad_out, positions, views, adjacency):
    rows, width = q_in.shape
    xs = parts // 2
    group = width // HD // parts
    chips = seqs * xs
    block = rows * parts
    span = count_span(adjacency.shape[0], seqs)
    tokens = seqs * block
    wide = 2 * block
    standing = STANDING.get(chips, tuple(range(chips)))
    head_of = [((c % xs) * 2 + (c // xs) % 2) * group + c // xs // 2 for c in standing]
    limits = pltpu.CompilerParams(vmem_limit_bytes=VMEM_LIMIT)

    def row_first():
        return lax.axis_index("head")

    def core_of():
        return lax.rem(lax.axis_index("head"), 2)

    def slab_of():
        return lax.axis_index("seq") // 2

    steps = inverse_steps()
    loaded = (positions, jnp.asarray(steps), q_in, k_in, v_in, grad_out)
    sent, table = pl.pallas_call(
        functools.partial(prepare_kernel, row_first, head_of),
        out_shape=(
            jax.ShapeDtypeStruct((chips, 4 * rows, HD), jnp.bfloat16),
            jax.ShapeDtypeStruct((2, block, HD), jnp.float32),
        ),
        in_specs=[whole(pltpu.HBM)] * 6,
        out_specs=(whole(), whole()),
        scratch_shapes=[
            pltpu.VMEM(positions.shape, jnp.int32),
            pltpu.VMEM(steps.shape, jnp.float32),
            *[pltpu.VMEM((rows, width), jnp.bfloat16)] * 4,
            pltpu.SemaphoreType.DMA((6,)),
        ],
        compiler_params=limits,
        name="prepare",
    )(*[pltpu.with_memory_space_constraint(x, pltpu.HBM) for x in loaded])
    axes = ("seq", "head")
    same_core = [[(c // xs) * parts + (c % xs) * 2 + core for c in standing] for core in range(2)]
    mine = lax.all_to_all(sent, axes, 0, 0, axis_index_groups=same_core, tiled=True)
    other = lax.ppermute(mine, axes, [(d, d ^ 1) for d in range(seqs * parts)])
    back = pl.pallas_call(
        functools.partial(attend_kernel, core_of, slab_of, standing),
        out_shape=jax.ShapeDtypeStruct((group, 4, block, HD), jnp.bfloat16),
        in_specs=[whole(pltpu.SMEM), whole(pltpu.SMEM), whole(), whole()],
        out_specs=whole(),
        scratch_shapes=[
            pltpu.VMEM((tokens, HD), jnp.bfloat16),
            pltpu.VMEM((tokens, HD), jnp.bfloat16),
            pltpu.VMEM((2 * tokens, HD), jnp.bfloat16),
            pltpu.VMEM((HD, tokens + (span - 1) * block), jnp.bfloat16),
            pltpu.VMEM((HD + 16, tokens + (span - 1) * block), jnp.bfloat16),
            pltpu.VMEM((HD, tokens), jnp.bfloat16),
            pltpu.VMEM((seqs // 2, span, block, wide), jnp.float32),
            pltpu.VMEM((seqs // 2, span * block, wide), jnp.bfloat16),
            pltpu.VMEM((seqs // 2, (span + 1) * block, wide), jnp.bfloat16),
            pltpu.VMEM((seqs // 2, (span + 1) * block, wide), jnp.bfloat16),
            pltpu.VMEM((HD, tokens), jnp.bfloat16),
            pltpu.VMEM((HD, tokens), jnp.bfloat16),
            *[pltpu.SMEM((seqs + 1,), jnp.int32)] * 3,
            pltpu.SMEM((chips,), jnp.int32),
        ],
        compiler_params=limits,
        name="attend",
    )(views, adjacency, mine, other)

    def route(m):
        pairs = []
        for d in range(seqs * parts):
            s, h = divmod(d, parts)
            to_s = ((s // 2) ^ m) * 2 + h % 2
            pairs.append((d, to_s * parts + h // 2 * 2 + s % 2))
        return pairs

    turns = [(group // 2 - n) % group for n in reversed(range(group))]
    chunks = [lax.ppermute(back[m], axes, route(m)) for m in turns]
    return pl.pallas_call(
        functools.partial(finish_kernel, slab_of, turns),
        out_shape=(jax.ShapeDtypeStruct((block, group * HD), jnp.bfloat16),) * 4,
        in_specs=[whole()] * (1 + group),
        out_specs=(whole(),) * 4,
        compiler_params=limits,
        name="finish",
    )(table, *chunks)


def solution(mesh):
    seqs, parts = mesh.shape["seq"], mesh.shape["head"]
    in_specs = (
        P(("seq", "head"), None),
        P(("seq", "head"), None),
        P(("seq", "head"), None),
        P(("seq", "head"), None),
        P(None, "seq"),
        P(),
        P(),
    )
    out_specs = (P("seq", "head"), P("seq", "head"), P("seq", "head"), P("seq", "head"))

    def run(*args):
        heads = args[0].shape[1] // HD
        count = args[6].shape[0]
        fits = (
            seqs * parts == 2 * heads
            and seqs % 2 == 0
            and parts % 2 == 0
            and seqs & (seqs - 1) == 0
            and count <= seqs < 2 * count
            and count_span(count, seqs) <= seqs
        )
        step = functools.partial(by_chip, seqs, parts) if fits else on_device
        return jax.shard_map(
            step, mesh=mesh, in_specs=in_specs, out_specs=out_specs, check_vma=False
        )(*args)

    return run
```

```python
import functools
import math

import jax
import jax.numpy as jnp
import numpy as np
from jax import lax
from jax.experimental import pallas as pl
from jax.experimental.pallas import tpu as pltpu
from jax.sharding import PartitionSpec as P

HD = 128


NEG = -1e30
THETA = 10000.0


def rope_tables(positions, width):
    side = width // 6 * 2
    first = width - 2 * side
    parts = []
    for row, group in ((0, first), (1, side), (2, side)):
        steps = jnp.arange(group // 2, dtype=jnp.float32)
        inverse = THETA ** (-2.0 * steps / group)
        parts.append(positions[row].astype(jnp.float32)[:, None] * inverse[None, :])
    angles = jnp.concatenate(parts, axis=1)
    return (jnp.cos(angles), jnp.sin(angles))


def rotate(values, cosine, sine, sign):
    half = values.shape[-1] // 2
    first = values[..., :half]
    second = values[..., half:]
    return jnp.concatenate(
        [first * cosine - sign * second * sine, sign * first * sine + second * cosine], axis=-1
    )


def neighbours(view_ids, adjacency):
    count = adjacency.shape[0]
    match = view_ids[:, None] == jnp.arange(count, dtype=jnp.int32)[None, :]
    near_one = jnp.sum(jnp.where(match, adjacency[None, :, 0], 0), axis=1)
    near_two = jnp.sum(jnp.where(match, adjacency[None, :, 1], 0), axis=1)
    return (near_one, near_two)


def in_blocks(pieces, carry, step):
    count = pieces[0].shape[0]
    size = count
    while size > 1024 and size % 2 == 0:
        size = size // 2
    number = count // size
    shaped = tuple((piece.reshape((number, size) + piece.shape[1:]) for piece in pieces))
    firsts = size * jnp.arange(number, dtype=jnp.int32)

    def advance(state, item):
        return (step(state, item[0], item[1]), None)

    final, _ = lax.scan(advance, carry, (shaped, firsts))
    return final


def on_device(q_in, k_in, v_in, grad_out, positions, views, adjacency):
    query, keys, values, grads = (
        lax.all_to_all(q_in, "head", split_axis=1, concat_axis=0, tiled=True),
        lax.all_to_all(k_in, "head", split_axis=1, concat_axis=0, tiled=True),
        lax.all_to_all(v_in, "head", split_axis=1, concat_axis=0, tiled=True),
        lax.all_to_all(grad_out, "head", split_axis=1, concat_axis=0, tiled=True),
    )
    rows, width = query.shape
    heads = width // HD
    scale = HD ** (-0.5)
    cosine, sine = rope_tables(positions, HD)
    cosine = cosine[:, None, :]
    sine = sine[:, None, :]
    query_rot = rotate(
        query.reshape(rows, heads, HD).astype(jnp.float32), cosine, sine, 1.0
    ).astype(jnp.bfloat16)
    key_rot = rotate(keys.reshape(rows, heads, HD).astype(jnp.float32), cosine, sine, 1.0).astype(
        jnp.bfloat16
    )
    value_split = values.reshape(rows, heads, HD)
    grad_split = grads.reshape(rows, heads, HD)
    first_row = lax.axis_index("seq") * rows
    own_views = lax.dynamic_slice_in_dim(views, first_row, rows)
    near_one, near_two = neighbours(own_views, adjacency)
    every_one, every_two = neighbours(views, adjacency)

    def allowed_keys(start, count):
        other = lax.dynamic_slice_in_dim(views, start, count)[None, :]
        return (
            (other == own_views[:, None])
            | (other == near_one[:, None])
            | (other == near_two[:, None])
        )

    def scores_for(key_block, allow):
        scores = (
            jnp.einsum("qhd,khd->hqk", query_rot, key_block, preferred_element_type=jnp.float32)
            * scale
        )
        return jnp.where(allow[None], scores, NEG)

    def soft_update(top, total, accum, block, start):
        key_block, value_block = block
        allow = allowed_keys(start, key_block.shape[0])
        scores = scores_for(key_block, allow)
        new_top = jnp.maximum(top, jnp.max(scores, axis=2))
        shrink = jnp.exp(top - new_top)
        weights = jnp.where(allow[None], jnp.exp(scores - new_top[..., None]), 0.0)
        total = total * shrink + jnp.sum(weights, axis=2)
        accum = accum * shrink[..., None] + jnp.einsum(
            "hqk,khd->hqd",
            weights.astype(jnp.bfloat16),
            value_block,
            preferred_element_type=jnp.float32,
        )
        return (new_top, total, accum, weights, shrink)

    top_init = jnp.full((heads, rows), NEG, jnp.float32)
    total_init = jnp.zeros((heads, rows), jnp.float32)
    accum_init = jnp.zeros((heads, rows, HD), jnp.float32)

    def step(inner, block, bstart):
        top, total, accum, weights, shrink = soft_update(
            inner[0], inner[1], inner[2], block, bstart
        )
        return (top, total, accum)

    top, total, accum = in_blocks(
        (
            lax.all_gather(key_rot, "seq", axis=0, tiled=True),
            lax.all_gather(value_split, "seq", axis=0, tiled=True),
        ),
        (top_init, total_init, accum_init),
        step,
    )
    output = accum / total[..., None]
    finish_level = top + jnp.log(total)
    finish_delta = jnp.sum(
        grad_split.astype(jnp.float32) * jnp.transpose(output, (1, 0, 2)), axis=2
    ).T
    output, level, delta = (output, finish_level, finish_delta)

    def step(inner, block, bstart):
        key_block, value_block = block
        allow = allowed_keys(bstart, key_block.shape[0])
        scores = scores_for(key_block, allow)
        probs = jnp.where(allow[None], jnp.exp(scores - level[..., None]), 0.0)
        dprobs = jnp.einsum(
            "qhd,khd->hqk", grad_split, value_block, preferred_element_type=jnp.float32
        )
        dscores = (probs * (dprobs - delta[..., None])).astype(jnp.bfloat16)
        return inner + jnp.einsum(
            "hqk,khd->hqd", dscores, key_block, preferred_element_type=jnp.float32
        )

    grad_query = (
        in_blocks(
            (
                lax.all_gather(key_rot, "seq", axis=0, tiled=True),
                lax.all_gather(value_split, "seq", axis=0, tiled=True),
            ),
            accum_init,
            step,
        )
        * scale
    )
    level_all, delta_all = (
        lax.all_gather(level.T, "seq", axis=0, tiled=True),
        lax.all_gather(delta.T, "seq", axis=0, tiled=True),
    )

    def step(inner, block, bstart):
        grad_key, grad_value = inner
        query_block, grad_block = block
        count = query_block.shape[0]
        query_views = lax.dynamic_slice_in_dim(views, bstart, count)[None, :]
        query_one = lax.dynamic_slice_in_dim(every_one, bstart, count)[None, :]
        query_two = lax.dynamic_slice_in_dim(every_two, bstart, count)[None, :]
        mine = own_views[:, None]
        allow = (mine == query_views) | (mine == query_one) | (mine == query_two)
        level_block = lax.dynamic_slice_in_dim(level_all, bstart, count).T
        delta_block = lax.dynamic_slice_in_dim(delta_all, bstart, count).T
        scores = (
            jnp.einsum("khd,qhd->hkq", key_rot, query_block, preferred_element_type=jnp.float32)
            * scale
        )
        probs = jnp.where(allow[None], jnp.exp(scores - level_block[:, None, :]), 0.0)
        grad_value = grad_value + jnp.einsum(
            "hkq,qhd->hkd",
            probs.astype(jnp.bfloat16),
            grad_block,
            preferred_element_type=jnp.float32,
        )
        dprobs = jnp.einsum(
            "khd,qhd->hkq", value_split, grad_block, preferred_element_type=jnp.float32
        )
        dscores = (probs * (dprobs - delta_block[:, None, :])).astype(jnp.bfloat16)
        grad_key = grad_key + jnp.einsum(
            "hkq,qhd->hkd", dscores, query_block, preferred_element_type=jnp.float32
        )
        return (grad_key, grad_value)

    grad_key, grad_value = in_blocks(
        (
            lax.all_gather(query_rot, "seq", axis=0, tiled=True),
            lax.all_gather(grad_split, "seq", axis=0, tiled=True),
        ),
        (accum_init, accum_init),
        step,
    )

    def token_major(stack):
        return jnp.transpose(stack, (1, 0, 2))

    attended = token_major(output).reshape(rows, width).astype(jnp.bfloat16)
    grad_q = (
        rotate(token_major(grad_query), cosine, sine, -1.0)
        .reshape(rows, width)
        .astype(jnp.bfloat16)
    )
    grad_k = (
        rotate(token_major(grad_key) * scale, cosine, sine, -1.0)
        .reshape(rows, width)
        .astype(jnp.bfloat16)
    )
    grad_v = token_major(grad_value).reshape(rows, width).astype(jnp.bfloat16)
    return (attended, grad_q, grad_k, grad_v)


LOG2E = math.log2(math.e)
VMEM_LIMIT = 48 * 1024 * 1024
STANDING = {16: (11, 13, 3, 2, 0, 6, 7, 5, 12, 1, 15, 10, 8, 9, 4, 14)}


def whole(space=pltpu.VMEM):
    return pl.BlockSpec(memory_space=space)


def inverse_steps():
    side = HD // 6 * 2
    first = HD - 2 * side
    parts, rows = [], []
    for row, group in ((0, first), (1, side), (2, side)):
        steps = np.arange(group // 2, dtype=np.float64)
        parts.append(THETA ** (-2.0 * steps / group))
        rows.append(np.full(group // 2, row))
    table = np.zeros((HD // 2, 8), np.float32)
    table[np.arange(HD // 2), np.concatenate(rows)] = np.concatenate(parts)
    return table


def prepare_kernel(
    row_first, head_of, pos_hbm, step_hbm, q_hbm, k_hbm, v_hbm, g_hbm, out_ref, table_ref,
    pos_ref, step_ref, q_ref, k_ref, v_ref, g_ref, sems,
):
    rows = q_ref.shape[0]
    pairs = (
        (pos_hbm, pos_ref), (step_hbm, step_ref), (q_hbm, q_ref), (k_hbm, k_ref), (v_hbm, v_ref), (g_hbm, g_ref)
    )
    copies = [pltpu.make_async_copy(src, dst, sems.at[i]) for i, (src, dst) in enumerate(pairs)]
    for copy in copies:
        copy.start()
    copies[0].wait()
    copies[1].wait()
    angle = (
        step_ref[:, 0:1] * pos_ref[0:1, :].astype(jnp.float32)
        + step_ref[:, 1:2] * pos_ref[1:2, :].astype(jnp.float32)
        + step_ref[:, 2:3] * pos_ref[2:3, :].astype(jnp.float32)
    )
    cosine, sine = jnp.cos(angle), jnp.sin(angle)
    table_ref[0] = jnp.concatenate([cosine, cosine], axis=0).T
    table_ref[1] = jnp.concatenate([-sine, sine], axis=0).T
    own = pl.ds(pl.multiple_of(row_first() * rows, rows), rows)
    cosine, sine = table_ref[0, own, :], table_ref[1, own, :]
    for copy in copies[2:]:
        copy.wait()
    for chip, head in enumerate(head_of):
        lanes = slice(head * HD, (head + 1) * HD)
        for at, ref in ((0, q_ref), (1, k_ref)):
            x = ref[:, lanes].astype(jnp.float32)
            out_ref[chip, at * rows : (at + 1) * rows, :] = (
                x * cosine + pltpu.roll(x, HD // 2, 1) * sine
            ).astype(jnp.bfloat16)
        out_ref[chip, 2 * rows : 3 * rows, :] = v_ref[:, lanes]
        out_ref[chip, 3 * rows : 4 * rows, :] = g_ref[:, lanes]


def attend_kernel(
    core_of, slab_of, standing, views_ref, near_ref, mine_ref, other_ref, out_ref,
    q_all, g_all, kv_all, kt_all, vt_all, gt_all, s_all, e_all, p_all, ds_all, at_all, dq_all,
    order, rank, place_of, stand_of,
):
    blocks = mine_ref.shape[0] // 2
    rows = mine_ref.shape[1] // 4
    block = 4 * rows
    count = near_ref.shape[0]
    span = count_span(count, blocks)
    long = blocks - 1 + span
    wide = 2 * block
    core, slab = core_of(), slab_of()
    scale = HD**-0.5
    factor = scale * LOG2E
    first, held = [], []
    for view in range(count):
        below, equal = 0, 0
        for b in range(blocks):
            below = below + (views_ref[b * block] < view).astype(jnp.int32)
            equal = equal + (views_ref[b * block] == view).astype(jnp.int32)
        first.append(below)
        held.append(equal)

    def pick(table, at):
        value = table[0]
        for view in range(1, count):
            value = jnp.where(at == view, table[view], value)
        return value

    last, now, place = jnp.int32(0), near_ref[0, 0], jnp.int32(0)
    start, size = [], []
    cycle = [last, now]
    for _ in range(count - 2):
        one, two = near_ref[now, 0], near_ref[now, 1]
        last, now = now, jnp.where(one == last, two, one)
        cycle.append(now)
    for i, view in enumerate(cycle):
        f, n = pick(first, view), pick(held, view)
        start.append(place)
        size.append(n)
        for extra in range(2):
            order[place + extra] = f + extra
            rank[place + extra] = jnp.int32(i)
        place = place + n

    nt = (((1,), (1,)), ((), ()))
    eye = (
        lax.broadcasted_iota(jnp.int32, (HD, HD), 0) == lax.broadcasted_iota(jnp.int32, (HD, HD), 1)
    ).astype(jnp.bfloat16)

    def turn(x):
        return lax.dot_general(eye, x, nt, preferred_element_type=jnp.float32).astype(jnp.bfloat16)

    def flip(x):
        return x.astype(jnp.float32).T.astype(jnp.bfloat16)

    for n, chip in enumerate(standing):
        stand_of[chip] = jnp.int32(n)
    for pos in range(blocks):
        src = order[pos]
        place_of[src] = jnp.int32(pos)
        here = slice(pos * block, (pos + 1) * block)
        for at, ref, base in (
            (0, q_all, pos * block), (1, kv_all, 2 * pos * block), (2, kv_all, (2 * pos + 1) * block), (3, g_all, pos * block)
        ):
            part = slice(at * rows, (at + 1) * rows)
            for x in range(2):
                n = stand_of[2 * src + x]
                for whose, c in ((mine_ref, core), (other_ref, 1 - core)):
                    to = pl.ds(pl.multiple_of(base + (2 * x + c) * rows, rows), rows)
                    ref[to, :] = whose[n, part, :]
        turned = turn(kv_all[2 * pos * block : 2 * (pos + 1) * block, :])
        for spot in range(pos % blocks, long, blocks):
            there = slice(spot * block, (spot + 1) * block)
            kt_all[:, there] = turned[:, :block]
            vt_all[:HD, there] = turned[:, block:]
        gt_all[:, here] = flip(g_all[here, :])
    vt_all[HD:, :] = jnp.ones((vt_all.shape[0] - HD, vt_all.shape[1]), jnp.bfloat16)

    second = lax.broadcasted_iota(jnp.int32, (1, wide), 1) >= block
    tiles = range(blocks // 2)
    lanes = [slice(tile * wide, (tile + 1) * wide) for tile in tiles]
    begins, ats, places, windows, oks = [], [], [], [], []
    for tile in tiles:
        rank_a, rank_b = rank[2 * tile], rank[2 * tile + 1]
        before = lax.rem(rank_a + count - 1, count)
        begin = lax.rem(pick(start, rank_a) - pick(size, before) + blocks, blocks)
        begins.append(begin)
        windows.append(pl.ds(pl.multiple_of(begin * block, block), span * block))
        at = [lax.rem(begin + i, blocks) for i in range(span)]
        places.append([pl.multiple_of(n * (2 * block), block) for n in at])
        oks.append([])
        for n in at:
            far_a = lax.rem(rank[n] - rank_a + count, count)
            far_b = lax.rem(rank[n] - rank_b + count, count)
            ok_a = ((far_a <= 1) | (far_a == count - 1)).astype(jnp.int32)
            ok_b = ((far_b <= 1) | (far_b == count - 1)).astype(jnp.int32)
            oks[tile].append(jnp.where(second, ok_b, ok_a) > 0)
    slabs = out_ref.shape[0]
    owned = [place_of[2 * jnp.bitwise_xor(slab, m) + core] for m in range(slabs)]
    levels, shares, deltas, sums = {}, {}, {}, [0, 0]

    def scores(tile):
        top = jnp.full((1, wide), NEG, jnp.float32)
        for i in range(span):
            s = lax.dot_general(
                kv_all[pl.ds(places[tile][i], block), :], q_all[lanes[tile], :], nt, preferred_element_type=jnp.float32
            )
            s_all[tile, i] = s
            top = jnp.maximum(top, jnp.where(oks[tile][i], jnp.max(s, axis=0, keepdims=True), NEG))
        levels[tile] = top * factor

    def weights(tile):
        for i in range(span):
            e = jnp.exp2(s_all[tile, i] * factor - jnp.where(oks[tile][i], levels[tile], -NEG))
            e_all[tile, i * block : (i + 1) * block, :] = e.astype(jnp.bfloat16)

    def outputs(tile):
        out = jnp.dot(vt_all[:, windows[tile]], e_all[tile], preferred_element_type=jnp.float32)
        total = out[HD : HD + 1, :]
        shares[tile] = 1.0 / total
        out = out[:HD, :] * shares[tile]
        at_all[:, lanes[tile]] = out.astype(jnp.bfloat16)
        deltas[tile] = jnp.sum(gt_all[:, lanes[tile]].astype(jnp.float32) * out, axis=0, keepdims=True)

    def slopes(tile):
        for i in range(span):
            here = slice(i * block, (i + 1) * block)
            d = lax.dot_general(
                kv_all[pl.ds(places[tile][i] + block, block), :], g_all[lanes[tile], :], nt, preferred_element_type=jnp.float32
            )
            p = e_all[tile, here, :].astype(jnp.float32) * shares[tile]
            p_all[tile, here, :] = p.astype(jnp.bfloat16)
            ds_all[tile, here, :] = (p * (d - deltas[tile])).astype(jnp.bfloat16)
        p_all[tile, span * block :, :] = jnp.zeros((block, wide), jnp.bfloat16)
        ds_all[tile, span * block :, :] = jnp.zeros((block, wide), jnp.bfloat16)

    def query_slopes(tile):
        dq = jnp.dot(kt_all[:, windows[tile]], ds_all[tile, : span * block, :], preferred_element_type=jnp.float32)
        dq_all[:, lanes[tile]] = (dq * scale).astype(jnp.bfloat16)

    def key_slopes(tile):
        rels = [
            pl.multiple_of(jnp.minimum(lax.rem(pos - begins[tile] + blocks, blocks), span) * block, block)
            for pos in owned
        ]
        for n, (ref, other) in enumerate(((ds_all, q_all), (p_all, g_all))):
            x = jnp.concatenate([ref[tile, pl.ds(rel, block), :] for rel in rels], axis=0)
            sums[n] = sums[n] + jnp.dot(x, other[lanes[tile], :], preferred_element_type=jnp.float32)

    scores(0)
    weights(0)
    scores(1)
    weights(1)
    scores(2)
    weights(2)
    scores(3)
    weights(3)
    outputs(0)
    outputs(1)
    outputs(2)
    outputs(3)
    slopes(0)
    slopes(1)
    slopes(2)
    slopes(3)
    query_slopes(0)
    query_slopes(1)
    query_slopes(2)
    query_slopes(3)
    key_slopes(0)
    key_slopes(1)
    key_slopes(2)
    key_slopes(3)
    dk, dv = sums
    for m, pos in enumerate(owned):
        here = pl.ds(pl.multiple_of(pos * block, block), block)
        out_ref[m, 0] = flip(at_all[:, here])
        out_ref[m, 1] = flip(dq_all[:, here])
        out_ref[m, 2] = (dk[m * block : (m + 1) * block] * scale).astype(jnp.bfloat16)
        out_ref[m, 3] = dv[m * block : (m + 1) * block].astype(jnp.bfloat16)


def finish_kernel(slab_of, turns, table_ref, *refs):
    chunks, outs = refs[:-4], refs[-4:]
    slab = slab_of()
    cosine, sine = table_ref[0], table_ref[1]
    for m, ref in zip(turns, chunks, strict=True):
        head = jnp.bitwise_xor(slab, m)
        lanes = pl.ds(pl.multiple_of(head * HD, HD), HD)
        for at, out in enumerate(outs):
            x = ref[at]
            if at in (1, 2):
                x = x.astype(jnp.float32)
                x = x * cosine - pltpu.roll(x, HD // 2, 1) * sine
                x = x.astype(jnp.bfloat16)
            out[:, lanes] = x


def count_span(count, blocks):
    return 4 + blocks - count


def by_chip(seqs, parts, q_in, k_in, v_in, grad_out, positions, views, adjacency):
    rows, width = q_in.shape
    xs = parts // 2
    group = width // HD // parts
    chips = seqs * xs
    block = rows * parts
    span = count_span(adjacency.shape[0], seqs)
    tokens = seqs * block
    wide = 2 * block
    standing = STANDING.get(chips, tuple(range(chips)))
    head_of = [((c % xs) * 2 + (c // xs) % 2) * group + c // xs // 2 for c in standing]
    limits = pltpu.CompilerParams(vmem_limit_bytes=VMEM_LIMIT)

    def row_first():
        return lax.axis_index("head")

    def core_of():
        return lax.rem(lax.axis_index("head"), 2)

    def slab_of():
        return lax.axis_index("seq") // 2

    steps = inverse_steps()
    loaded = (positions, jnp.asarray(steps), q_in, k_in, v_in, grad_out)
    sent, table = pl.pallas_call(
        functools.partial(prepare_kernel, row_first, head_of),
        out_shape=(
            jax.ShapeDtypeStruct((chips, 4 * rows, HD), jnp.bfloat16),
            jax.ShapeDtypeStruct((2, block, HD), jnp.float32),
        ),
        in_specs=[whole(pltpu.HBM)] * 6,
        out_specs=(whole(), whole()),
        scratch_shapes=[
            pltpu.VMEM(positions.shape, jnp.int32),
            pltpu.VMEM(steps.shape, jnp.float32),
            *[pltpu.VMEM((rows, width), jnp.bfloat16)] * 4,
            pltpu.SemaphoreType.DMA((6,)),
        ],
        compiler_params=limits,
        name="prepare",
    )(*[pltpu.with_memory_space_constraint(x, pltpu.HBM) for x in loaded])
    axes = ("seq", "head")
    same_core = [[(c // xs) * parts + (c % xs) * 2 + core for c in standing] for core in range(2)]
    mine = lax.all_to_all(sent, axes, 0, 0, axis_index_groups=same_core, tiled=True)
    other = lax.ppermute(mine, axes, [(d, d ^ 1) for d in range(seqs * parts)])
    back = pl.pallas_call(
        functools.partial(attend_kernel, core_of, slab_of, standing),
        out_shape=jax.ShapeDtypeStruct((group, 4, block, HD), jnp.bfloat16),
        in_specs=[whole(pltpu.SMEM), whole(pltpu.SMEM), whole(), whole()],
        out_specs=whole(),
        scratch_shapes=[
            pltpu.VMEM((tokens, HD), jnp.bfloat16),
            pltpu.VMEM((tokens, HD), jnp.bfloat16),
            pltpu.VMEM((2 * tokens, HD), jnp.bfloat16),
            pltpu.VMEM((HD, tokens + (span - 1) * block), jnp.bfloat16),
            pltpu.VMEM((HD + 16, tokens + (span - 1) * block), jnp.bfloat16),
            pltpu.VMEM((HD, tokens), jnp.bfloat16),
            pltpu.VMEM((seqs // 2, span, block, wide), jnp.float32),
            pltpu.VMEM((seqs // 2, span * block, wide), jnp.bfloat16),
            pltpu.VMEM((seqs // 2, (span + 1) * block, wide), jnp.bfloat16),
            pltpu.VMEM((seqs // 2, (span + 1) * block, wide), jnp.bfloat16),
            pltpu.VMEM((HD, tokens), jnp.bfloat16),
            pltpu.VMEM((HD, tokens), jnp.bfloat16),
            *[pltpu.SMEM((seqs + 1,), jnp.int32)] * 3,
            pltpu.SMEM((chips,), jnp.int32),
        ],
        compiler_params=limits,
        name="attend",
    )(views, adjacency, mine, other)

    def route(m):
        pairs = []
        for d in range(seqs * parts):
            s, h = divmod(d, parts)
            to_s = ((s // 2) ^ m) * 2 + h % 2
            pairs.append((d, to_s * parts + h // 2 * 2 + s % 2))
        return pairs

    turns = [(group // 2 - n) % group for n in reversed(range(group))]
    chunks = [lax.ppermute(back[m], axes, route(m)) for m in turns]
    return pl.pallas_call(
        functools.partial(finish_kernel, slab_of, turns),
        out_shape=(jax.ShapeDtypeStruct((block, group * HD), jnp.bfloat16),) * 4,
        in_specs=[whole()] * (1 + group),
        out_specs=(whole(),) * 4,
        compiler_params=limits,
        name="finish",
    )(table, *chunks)


def solution(mesh):
    seqs, parts = mesh.shape["seq"], mesh.shape["head"]
    in_specs = (
        P(("seq", "head"), None),
        P(("seq", "head"), None),
        P(("seq", "head"), None),
        P(("seq", "head"), None),
        P(None, "seq"),
        P(),
        P(),
    )
    out_specs = (P("seq", "head"), P("seq", "head"), P("seq", "head"), P("seq", "head"))

    def run(*args):
        heads = args[0].shape[1] // HD
        count = args[6].shape[0]
        fits = (
            seqs * parts == 2 * heads
            and seqs % 2 == 0
            and parts % 2 == 0
            and count <= seqs < 2 * count
            and count_span(count, seqs) <= seqs
        )
        step = functools.partial(by_chip, seqs, parts) if fits else on_device
        return jax.shard_map(
            step, mesh=mesh, in_specs=in_specs, out_specs=out_specs, check_vma=False
        )(*args)

    return run
```
